256 devices in a mesh: tok: 32 (over x, y, core), head: 8 (over z).
Axes of the slice: x: 4, y: 4, z: 8, core: 2. Of those that a mesh axis runs over, the one named last changes fastest.
Arguments:
- queries: bfloat16 [8192, 32, 128], P(('tok', 'head')), may hold values from -8 to 8
- keys: bfloat16 [8192, 8, 128], P(('tok', 'head')), may hold values from -8 to 8
- values: bfloat16 [8192, 8, 128], P(('tok', 'head')), may hold values from -6 to 6
- grad_out: bfloat16 [8192, 32, 128], P(('tok', 'head')), may hold values from -6 to 6
- ancestry: int32 [64, 16], replicated, may hold values from -1 to 63, as said below
Outputs:
- grad_queries: bfloat16 [8192, 32, 128], P(('tok', 'head'))
- grad_keys: bfloat16 [8192, 8, 128], P(('tok', 'head'))
- grad_values: bfloat16 [8192, 8, 128], P(('tok', 'head'))
The draws below stay inside these ranges and needn't reach their ends.
Inputs may be any that keep to these rules, and one draw needn't show every extreme that they name: `ancestry`: row a lists the ancestor blocks of block a, nearest first, then -1 entries. Every ancestor is a block of the same tok index as a (same index // 2) or the first block of some tok index (an index that is a multiple of 2). Some block has exactly 16 ancestors.
All inputs are finite; a program needn't handle non-finite values.
Results may differ from the reference program's by a relative error of at most 0.0097.
Values may be sent and summed in bfloat16 or wider, within the bound.
A program may use at most 64 MiB of HBM per device.

```python
import math
import jax
import jax.numpy as jnp
from jax import lax

HD = 128
QH = 32
KVH = 8
BLK = 128
TOK_DEV = 256
TOKENS = 8192
PROMPT = 16
DEPTH = 16
N_TOK = 32


def draw_queries(key, part):
    key = jax.random.fold_in(key, 21)
    entries = jax.random.normal(key, (TOKENS, QH, HD), jnp.float32)
    return jnp.clip(entries, -8.0, 8.0).astype(jnp.bfloat16)


def draw_keys(key, part):
    key = jax.random.fold_in(key, 33)
    entries = jax.random.normal(key, (TOKENS, KVH, HD), jnp.float32)
    return jnp.clip(entries, -8.0, 8.0).astype(jnp.bfloat16)


def draw_ancestry(key, part):
    key = jax.random.fold_in(key, 7)
    sub_keys = jax.random.split(key, 6)
    per_dev = TOK_DEV // BLK
    device_ids = jnp.arange(N_TOK, dtype=jnp.int32)
    window = jax.random.randint(sub_keys[0], (), 0, N_TOK // PROMPT)
    random_cut = jax.random.randint(sub_keys[1], (N_TOK,), 0, 4) == 0
    inside = (device_ids // PROMPT == window) & (device_ids % PROMPT != 0)
    cuts = (device_ids % PROMPT == 0) | random_cut & jnp.logical_not(inside)
    starts = lax.cummax(jnp.where(cuts, device_ids, 0), axis=0)
    prompt_depth = device_ids - starts
    deepest = window * PROMPT + PROMPT - 1
    lead_parent = jnp.where(prompt_depth > 0, (device_ids - 1) * per_dev, -1)
    slot_ids = jnp.arange(per_dev, dtype=jnp.int32)
    chained = (jax.random.randint(sub_keys[2], (N_TOK, per_dev), 0, 2) == 1) & (slot_ids[None, :] >= 2)
    target = jax.random.randint(sub_keys[3], (N_TOK, per_dev), 0, N_TOK)
    heavy = jax.random.randint(sub_keys[4], (N_TOK,), 0, 4) == 0
    forced = jax.random.randint(sub_keys[5], (), 0, N_TOK)
    heavy = heavy | (device_ids == forced)
    target = jnp.where(heavy[:, None], deepest, target)
    chained = jnp.where(heavy[:, None], slot_ids[None, :] >= 2, chained)
    own_ids = device_ids[:, None] * per_dev + slot_ids[None, :]
    parent = jnp.where(chained, own_ids - 1, target * per_dev)
    parent = jnp.where(slot_ids[None, :] == 0, lead_parent[:, None], parent)
    parent = parent.reshape(-1).astype(jnp.int32)
    current = parent
    columns = []
    for level in range(DEPTH):
        columns.append(current)
        current = jnp.where(current >= 0, parent[jnp.maximum(current, 0)], -1).astype(jnp.int32)
    return jnp.stack(columns, axis=1).astype(jnp.int32)


def steps_of(stream_key, shape, pieces, least, largest):
    gain = 1.0
    for dim, shards_of in pieces:
        draws = jax.random.uniform(jax.random.fold_in(jax.random.fold_in(stream_key, 6), dim), (shards_of,), jnp.float32, least / len(pieces), largest / len(pieces))
        gain = gain * jnp.repeat(jnp.exp(draws), shape[dim] // shards_of).reshape((-1,) + (1,) * (len(shape) - 1 - dim))
    return gain


def gaussian(key, dims, width, bound, cuts=(), kind=jnp.bfloat16):
    values = width * jax.random.normal(key, dims, jnp.float32)
    if cuts:
        values = values * steps_of(key, dims, cuts, -0.22, 0.18)
    return jnp.clip(values, -bound, bound).astype(kind)


def setup_inputs(seed: int = 0) -> dict:
    seeds = jax.random.split(jax.random.key(seed), 6)
    return {
        "queries": draw_queries(jax.random.fold_in(seeds[5], 71), 0),
        "keys": draw_keys(jax.random.fold_in(seeds[5], 71), 0),
        "values": gaussian(seeds[2], (TOKENS, KVH, HD), 1.0, 6.0, ((0, 256),)),
        "grad_out": gaussian(seeds[3], (TOKENS, QH, HD), 1.0, 6.0, ((0, 256),)),
        "ancestry": draw_ancestry(jax.random.fold_in(seeds[5], 71), 0),
    }


def reference(queries, keys, values, grad_out, ancestry):
    block_count = queries.shape[0] // BLK
    key_heads = keys.shape[1]
    group_size = queries.shape[1] // key_heads
    factor = 1.0 / math.sqrt(HD)
    query_blocks = queries.reshape(block_count, BLK, key_heads, group_size, HD)
    grad_blocks = grad_out.reshape(block_count, BLK, key_heads, group_size, HD)
    key_blocks = keys.reshape(block_count, BLK, key_heads, HD)
    value_blocks = values.reshape(block_count, BLK, key_heads, HD)
    chains = jnp.concatenate([jnp.arange(block_count, dtype=jnp.int32)[:, None], ancestry.astype(jnp.int32)], axis=1)
    slot_count = chains.shape[1]
    col_index = jnp.arange(slot_count * BLK)
    col_slot = col_index // BLK
    col_row = col_index % BLK
    row_index = jnp.arange(BLK)

    def one_block(state, block_id):
        key_grads, value_grads = state
        chain_ids = chains[block_id]
        live_mask = chain_ids >= 0
        where_at = jnp.where(live_mask, chain_ids, 0).astype(jnp.int32)
        key_rows = key_blocks[where_at].reshape(slot_count * BLK, key_heads, HD).astype(jnp.float32)
        value_rows = value_blocks[where_at].reshape(slot_count * BLK, key_heads, HD).astype(jnp.float32)
        query_rows = query_blocks[block_id].astype(jnp.float32)
        grad_rows = grad_blocks[block_id].astype(jnp.float32)
        scores = jnp.einsum('igpd,jgd->gpij', query_rows, key_rows) * factor
        visible = live_mask[col_slot][None, :] & ((col_slot[None, :] > 0) | (col_row[None, :] <= row_index[:, None]))
        scores = jnp.where(visible, scores, -jnp.inf)
        row_max = lax.optimization_barrier(jnp.max(scores, axis=-1, keepdims=True))
        exponent = jnp.exp(scores - row_max)
        probs = exponent / lax.optimization_barrier(jnp.sum(exponent, axis=-1, keepdims=True))
        probs_b = lax.optimization_barrier(probs.astype(jnp.bfloat16)).astype(jnp.float32)
        attended = jnp.einsum('gpij,jgd->igpd', probs_b, value_rows)
        delta_row = jnp.transpose(lax.optimization_barrier(jnp.sum(grad_rows * attended, axis=-1)), (1, 2, 0))
        dprobs = jnp.einsum('igpd,jgd->gpij', grad_rows, value_rows)
        dscores = probs * (dprobs - delta_row[..., None])
        dscores_b = lax.optimization_barrier(dscores.astype(jnp.bfloat16)).astype(jnp.float32)
        query_grad = (jnp.einsum('gpij,jgd->igpd', dscores_b, key_rows) * factor).astype(jnp.bfloat16)
        key_part = jnp.einsum('gpij,igpd->jgd', dscores_b, query_rows) * factor
        value_part = jnp.einsum('gpij,igpd->jgd', probs_b, grad_rows)
        key_grads = key_grads.at[where_at].add(key_part.reshape(slot_count, BLK, key_heads, HD))
        value_grads = value_grads.at[where_at].add(value_part.reshape(slot_count, BLK, key_heads, HD))
        return ((key_grads, value_grads), query_grad)
    empty = jnp.zeros((block_count, BLK, key_heads, HD), jnp.float32)
    (key_grads, value_grads), query_grad = lax.scan(one_block, (empty, empty), jnp.arange(block_count, dtype=jnp.int32))
    grad_queries = query_grad.reshape(queries.shape)
    grad_keys = key_grads.reshape(keys.shape).astype(jnp.bfloat16)
    grad_values = value_grads.reshape(values.shape).astype(jnp.bfloat16)
    return (grad_queries, grad_keys, grad_values)
```

```python
import functools
import math

import jax
import jax.numpy as jnp
from jax import lax
from jax.experimental import pallas as pl
from jax.experimental.pallas import tpu as pltpu
from jax.sharding import PartitionSpec as P

BLK = 128
HD = 128
GROUP = 4
HEADS = 8
NX, NY, NC = 4, 4, 2
NT = NX * NY * NC
SLICE = 32
DEPTH = 16
SLOTS = DEPTH + 1
ZERO_SLOT = SLOTS
POOL = NT + 1
ROWS = BLK * GROUP
FACTOR = 1.0 / math.sqrt(HD)
SCALE2 = FACTOR * math.log2(math.e)
HIDDEN = -1e30
GS = 2
Z_ORDER = (4, 3, 5, 2, 6, 1, 7)
VMEM_LIMIT = 48 * 1024 * 1024
MESH = pl.DeviceIdType.MESH


def remote(src, dst, send_sem, recv_sem, **where):
    return pltpu.make_async_remote_copy(
        src_ref=src,
        dst_ref=dst,
        send_sem=send_sem,
        recv_sem=recv_sem,
        device_id=where,
        device_id_type=MESH,
    )


def place():
    t = lax.axis_index("tok")
    return t, lax.axis_index("head"), t // (NY * NC), (t // NC) % NY, t % NC


def tok_at(x, y, c):
    return (x % NX) * (NY * NC) + (y % NY) * NC + c


def enter(t, z, x, y, c):
    barrier = pltpu.get_barrier_semaphore()
    for dz in range(1, HEADS):
        pl.semaphore_signal(barrier, inc=1, device_id={"head": (z + dz) % HEADS}, device_id_type=MESH)
    for d in range(1, NX):
        pl.semaphore_signal(barrier, inc=1, device_id={"tok": tok_at(x + d, y, c)}, device_id_type=MESH)
    for d in range(1, NY):
        pl.semaphore_signal(barrier, inc=1, device_id={"tok": tok_at(x, y + d, c)}, device_id_type=MESH)
    pl.semaphore_signal(barrier, inc=1, device_id={"tok": tok_at(x, y, 1 - c)}, device_id_type=MESH)
    pl.semaphore_wait(barrier, HEADS - 1 + NX - 1 + NY - 1 + 1)


def one_hot(source):
    rows = lax.broadcasted_iota(jnp.int32, (256, 256), 0)
    cols = lax.broadcasted_iota(jnp.int32, (256, 256), 1)
    return jnp.where(source(rows) == cols, 1.0, 0.0).astype(jnp.bfloat16)


def exact_dot(picks, rows):
    return jnp.dot(picks, rows, preferred_element_type=jnp.float32).astype(jnp.bfloat16)


def heads_first(i):
    return (i // 4 % 8) * 32 + (i // 32) * 4 + i % 4


def tokens_first(i):
    return (i // 4 % 8) * 32 + (i // 32) * 4 + i % 4


def kv_heads_first(i):
    return (i % 32) * 8 + i // 32


def kv_tokens_first(i):
    return (i % 8) * 32 + i // 8


def gather_kernel(
    anc_ref, q_ref, k_ref, v_ref, g_ref,
    qg_ref, pool_ref, chain_ref, inv_ref,
    qs, kvs, kv_send, kv_recv, qg_send, qg_recv,
    first_send, first_recv, second_send, second_recv, core_send, core_recv,
):
    t, z, x, y, c = place()
    picks = one_hot(kv_heads_first)
    kvs[:, 0] = exact_dot(picks, k_ref[...]).reshape(HEADS, SLICE, HD)
    kvs[:, 1] = exact_dot(picks, v_ref[...]).reshape(HEADS, SLICE, HD)
    half = z // 4
    slot = jnp.where(half == 0, t, NT)
    rows = pl.ds(pl.multiple_of((z % 4) * SLICE, SLICE), SLICE)
    pool_ref[slot, :, rows, :] = kvs[z]
    enter(t, z, x, y, c)

    kv_copies = []
    for dz in Z_ORDER:
        to = (z + dz) % HEADS
        copy = remote(kvs.at[to], pool_ref.at[slot, :, rows, :], kv_send.at[dz], kv_recv.at[dz], head=to)
        copy.start()
        kv_copies.append(copy)

    picks = one_hot(heads_first)
    for i, ref in enumerate((q_ref, g_ref)):
        for o in range(4):
            moved = exact_dot(picks, ref[o * 256 : (o + 1) * 256, :])
            qs[:, i, o * 32 : (o + 1) * 32, :] = moved.reshape(HEADS, 32, HD)
    qg_ref[z] = qs[z]
    qg_copies = []
    for dz in Z_ORDER:
        to = (z + dz) % HEADS
        copy = remote(qs.at[to], qg_ref.at[z], qg_send.at[dz], qg_recv.at[dz], head=to)
        copy.start()
        qg_copies.append(copy)

    for copy in kv_copies:
        copy.wait_recv()

    sends = []

    def step(i, d):
        return (x + d, y) if i == 0 else (x, y + d)

    def both(i, d, e):
        return (x + d, y + e) if i == 0 else (x + e, y + d)

    def second(i, d, e):
        from_slot = tok_at(*step(i, -d), c)
        to = tok_at(*both(i, 0, e), c)
        ref = pool_ref.at[from_slot, i]
        return remote(ref, ref, second_send.at[i, d, e], second_recv.at[i, d, e], tok=to)

    def across(i, d, e):
        ref = pool_ref.at[tok_at(*both(i, -d, -e), c), i]
        return remote(ref, ref, core_send.at[i, d, e], core_recv.at[i, d, e], tok=tok_at(x, y, 1 - c))

    def launch(copy):
        copy.start()
        sends.append(copy)

    mine = tok_at(x, y, c)
    firsts = []
    for d in (2, 1, 3):
        for i in range(2):
            ref = pool_ref.at[mine, i]
            copy = remote(ref, ref, first_send.at[i, d], first_recv.at[i, d], tok=tok_at(*step(i, d), c))
            launch(copy)
    for i in range(2):
        for e in (2, 1, 3):
            launch(second(i, 0, e))
    for i in range(2):
        launch(across(i, 0, 0))
    for d in (1, 3, 2):
        for i in range(2):
            ref = pool_ref.at[tok_at(*step(i, -d), c), i]
            remote(ref, ref, first_send.at[i, d], first_recv.at[i, d], tok=mine).wait_recv()
            for e in (2, 1, 3):
                launch(second(i, d, e))
            launch(across(i, d, 0))

    for b in range(2):
        chain_ref[b, 0] = t if b == 0 else jnp.int32(NT)
        chain_ref[b, SLOTS] = jnp.int32(0)
        for s in range(DEPTH):
            a = anc_ref[2 * t + b, s]
            chain_ref[b, 1 + s] = jnp.where(a < 0, -1, jnp.where(a % 2 == 1, NT, a // 2))

    @pl.loop(0, POOL)
    def _(p):
        for b in range(2):
            at = jnp.int32(ZERO_SLOT)
            for s in range(SLOTS):
                at = jnp.where(chain_ref[b, s] == p, s, at)
            inv_ref[b, p] = at

    for d in (0, 1, 3, 2):
        for e in (1, 3, 2):
            for i in range(2):
                ref = pool_ref.at[tok_at(*both(i, -d, -e), c), i]
                remote(ref, ref, second_send.at[i, d, e], second_recv.at[i, d, e], tok=mine).wait_recv()
                launch(across(i, d, e))
    for d in range(4):
        for e in range(4):
            for i in range(2):
                ref = pool_ref.at[tok_at(*both(i, -d, -e), 1 - c), i]
                remote(ref, ref, core_send.at[i, d, e], core_recv.at[i, d, e], tok=mine).wait_recv()
    for copy in qg_copies:
        copy.wait_recv()
    for copy in kv_copies + qg_copies + sends:
        copy.wait_send()


def fold(tile, op):
    return op(tile.reshape(-1, 8, ROWS), axis=0)


def attend_kernel(chain_ref, inv_ref, qg_ref, pool_ref, dq_ref, part_ref, qt, gt, score, dprob, parts):
    parts[:, ZERO_SLOT] = jnp.zeros((2, 2, BLK, HD), jnp.float32)
    for b in range(2):
        q = qg_ref[4 * b : 4 * b + 4, 0].reshape(ROWS, HD)
        g = qg_ref[4 * b : 4 * b + 4, 1].reshape(ROWS, HD)
        qt[...] = q.T
        gt[...] = g.T

        def tiles(first, count, i):
            found = [pool_ref[jnp.maximum(chain_ref[b, first + j], 0), i] for j in range(count)]
            return found[0] if count == 1 else jnp.concatenate(found, axis=0)

        def rows_of(first, count):
            return pl.ds(first * BLK, count * BLK)

        def look(first, count, top):
            s = jnp.dot(tiles(first, count, 0), qt[...], preferred_element_type=jnp.float32)
            for j in range(count):
                part = s[j * BLK : (j + 1) * BLK]
                if count == 1:
                    key = lax.broadcasted_iota(jnp.int32, (BLK, ROWS), 0)
                    row = lax.broadcasted_iota(jnp.int32, (BLK, ROWS), 1)
                    part = jnp.where(key * GROUP <= row, part, HIDDEN)
                else:
                    part = part + jnp.where(chain_ref[b, first + j] >= 0, 0.0, HIDDEN)
                score[rows_of(first + j, 1), :] = part
                top = jnp.maximum(top, fold(part, jnp.max))
            return top

        top = look(0, 1, jnp.full((8, ROWS), HIDDEN, jnp.float32))
        top = lax.fori_loop(0, DEPTH // GS, lambda n, top: look(1 + n * GS, GS, top), top)
        top = jnp.max(top, axis=0, keepdims=True) * SCALE2

        def weigh(first, count, sums):
            total, weighted = sums
            e = jnp.exp2(score[rows_of(first, count), :] * SCALE2 - top)
            dp = jnp.dot(tiles(first, count, 1), gt[...], preferred_element_type=jnp.float32)
            score[rows_of(first, count), :] = e
            dprob[rows_of(first, count), :] = dp
            return total + fold(e, jnp.sum), weighted + fold(e * dp, jnp.sum)

        zero = jnp.zeros((8, ROWS), jnp.float32)
        sums = weigh(0, 1, (zero, zero))
        total, weighted = lax.fori_loop(0, DEPTH // GS, lambda n, sums: weigh(1 + n * GS, GS, sums), sums)
        over = 1.0 / jnp.sum(total, axis=0, keepdims=True)
        delta = jnp.sum(weighted, axis=0, keepdims=True) * over

        def push(first, count, dqt):
            p = score[rows_of(first, count), :] * over
            ds = (p * (dprob[rows_of(first, count), :] - delta)).astype(jnp.bfloat16)
            dv = jnp.dot(p.astype(jnp.bfloat16), g, preferred_element_type=jnp.float32)
            dk = jnp.dot(ds, q, preferred_element_type=jnp.float32) * FACTOR
            for j in range(count):
                parts[b, first + j, 0] = dk[j * BLK : (j + 1) * BLK]
                parts[b, first + j, 1] = dv[j * BLK : (j + 1) * BLK]
            return dqt + lax.dot_general(
                tiles(first, count, 0), ds, (((0,), (0,)), ((), ())), preferred_element_type=jnp.float32
            )

        dqt = push(0, 1, jnp.zeros((HD, ROWS), jnp.float32))
        dqt = lax.fori_loop(0, DEPTH // GS, lambda n, dqt: push(1 + n * GS, GS, dqt), dqt)
        dq = (dqt * FACTOR).T.astype(jnp.bfloat16)
        dq_ref[4 * b : 4 * b + 4] = dq.reshape(4, SLICE * GROUP, HD)

    @pl.loop(0, POOL)
    def _(p):
        part_ref[p] = (parts[0, inv_ref[0, p]] + parts[1, inv_ref[1, p]]).astype(jnp.bfloat16)


def scatter_kernel(
    dq_ref, part_ref, gq_ref, gk_ref, gv_ref,
    dq_in, core_in, plane, second_in, line, first_in, home, home_in,
    dq_send, dq_recv, core_send, core_recv, second_send, second_recv,
    first_send, first_recv, home_send, home_recv,
):
    t, z, x, y, c = place()
    enter(t, z, x, y, c)
    core_copies = []
    for d in (1, 2, 3, 0):
        for n in range(NX):
            at = n * NY + (y + d) % NY
            copy = remote(
                part_ref.at[tok_at(n, y + d, 1 - c)], core_in.at[at], core_send.at[d, n], core_recv.at[d, n],
                tok=tok_at(x, y, 1 - c),
            )
            copy.start()
            core_copies.append(copy)
    dq_copies = []
    for dz in Z_ORDER:
        to = (z + dz) % HEADS
        copy = remote(dq_ref.at[to], dq_in.at[z], dq_send.at[dz], dq_recv.at[dz], head=to)
        copy.start()
        dq_copies.append(copy)
    dq_in[z] = dq_ref[z]

    for copy in core_copies:
        copy.wait_recv()

    @pl.loop(0, NX)
    def _(n):
        for m in range(NY):
            mine = part_ref[tok_at(n, m, c)].astype(jnp.float32)
            total = (mine + core_in[n * NY + m].astype(jnp.float32)).astype(jnp.bfloat16)
            plane[0, m, n] = total[0]
            plane[1, n, m] = total[1]

    spot = (y, x)
    second_copies = []
    for d in (2, 1, 3):
        for i in range(2):
            to = tok_at(x, y + d, c) if i == 0 else tok_at(x + d, y, c)
            copy = remote(
                plane.at[i, (spot[i] + d) % 4], second_in.at[i, d], second_send.at[i, d], second_recv.at[i, d], tok=to
            )
            copy.start()
            second_copies.append(copy)
    for copy in second_copies:
        copy.wait_recv()

    for i in range(2):
        total = plane[i, spot[i]].astype(jnp.float32)
        for d in range(1, 4):
            total = total + second_in[i, d].astype(jnp.float32)
        line[i] = total.astype(jnp.bfloat16)
    spot = (x, y)
    first_copies = []
    for d in (2, 1, 3):
        for i in range(2):
            to = tok_at(x + d, y, c) if i == 0 else tok_at(x, y + d, c)
            copy = remote(
                line.at[i, (spot[i] + d) % 4], first_in.at[i, d], first_send.at[i, d], first_recv.at[i, d], tok=to
            )
            copy.start()
            first_copies.append(copy)

    picks = one_hot(tokens_first)
    for copy in dq_copies:
        copy.wait_recv()
    for o in range(4):
        rows = dq_in[:, o * 32 : (o + 1) * 32, :].reshape(256, HD)
        gq_ref[o * 256 : (o + 1) * 256, :] = exact_dot(picks, rows)

    for copy in first_copies:
        copy.wait_recv()
    for i in range(2):
        total = line[i, spot[i]].astype(jnp.float32)
        for d in range(1, 4):
            total = total + first_in[i, d].astype(jnp.float32)
        home[0:4, i] = total.astype(jnp.bfloat16).reshape(4, SLICE, HD)
        home[4:8, i] = part_ref[NT, i].reshape(4, SLICE, HD)
    home_copies = []
    for dz in Z_ORDER:
        to = (z + dz) % HEADS
        copy = remote(home.at[to], home_in.at[z], home_send.at[dz], home_recv.at[dz], head=to)
        copy.start()
        home_copies.append(copy)
    home_in[z] = home[z]
    picks = one_hot(kv_tokens_first)
    for copy in home_copies:
        copy.wait_recv()
    gk_ref[...] = exact_dot(picks, home_in[:, 0].reshape(256, HD))
    gv_ref[...] = exact_dot(picks, home_in[:, 1].reshape(256, HD))
    for copy in core_copies + dq_copies + second_copies + first_copies + home_copies:
        copy.wait_send()


def whole():
    return pl.BlockSpec(memory_space=pltpu.VMEM)


def scalars():
    return pl.BlockSpec(memory_space=pltpu.SMEM)


def shape(*dims, dtype=jnp.bfloat16):
    return jax.ShapeDtypeStruct(dims, dtype)


def buffer(*dims, dtype=jnp.bfloat16):
    return pltpu.VMEM(dims, dtype)


def sems(*dims):
    return pltpu.SemaphoreType.DMA(dims)


def local(queries, keys, values, grad_out, ancestry):
    rows = SLICE * GROUP
    qg, pool, chain, inverse = pl.pallas_call(
        gather_kernel,
        out_shape=(
            shape(HEADS, 2, rows, HD),
            shape(POOL, 2, BLK, HD),
            shape(2, SLOTS + 1, dtype=jnp.int32),
            shape(2, POOL, dtype=jnp.int32),
        ),
        in_specs=[scalars()] + [whole()] * 4,
        out_specs=(whole(), whole(), scalars(), scalars()),
        scratch_shapes=[
            buffer(HEADS, 2, rows, HD),
            buffer(HEADS, 2, SLICE, HD),
            sems(8), sems(8), sems(8), sems(8),
            sems(2, 4), sems(2, 4), sems(2, 4, 4), sems(2, 4, 4), sems(2, 4, 4), sems(2, 4, 4),
        ],
        compiler_params=pltpu.CompilerParams(collective_id=0, has_side_effects=True, vmem_limit_bytes=VMEM_LIMIT),
        name="gather",
    )(
        ancestry,
        queries.reshape(SLICE * 32, HD),
        keys.reshape(SLICE * HEADS, HD),
        values.reshape(SLICE * HEADS, HD),
        grad_out.reshape(SLICE * 32, HD),
    )
    dq, part = pl.pallas_call(
        attend_kernel,
        out_shape=(shape(HEADS, rows, HD), shape(POOL, 2, BLK, HD)),
        in_specs=[scalars(), scalars(), whole(), whole()],
        out_specs=(whole(), whole()),
        scratch_shapes=[
            buffer(HD, ROWS),
            buffer(HD, ROWS),
            buffer(SLOTS * BLK, ROWS, dtype=jnp.float32),
            buffer(SLOTS * BLK, ROWS, dtype=jnp.float32),
            buffer(2, SLOTS + 1, 2, BLK, HD, dtype=jnp.float32),
        ],
        compiler_params=pltpu.CompilerParams(vmem_limit_bytes=VMEM_LIMIT),
        name="attend",
    )(chain, inverse, qg, pool)
    gq, gk, gv = pl.pallas_call(
        scatter_kernel,
        out_shape=(shape(SLICE * 32, HD), shape(SLICE * HEADS, HD), shape(SLICE * HEADS, HD)),
        in_specs=[whole(), whole()],
        out_specs=(whole(), whole(), whole()),
        scratch_shapes=[
            buffer(HEADS, rows, HD),
            buffer(16, 2, BLK, HD),
            buffer(2, 4, 4, BLK, HD),
            buffer(2, 4, 4, BLK, HD),
            buffer(2, 4, BLK, HD),
            buffer(2, 4, BLK, HD),
            buffer(HEADS, 2, SLICE, HD),
            buffer(HEADS, 2, SLICE, HD),
            sems(8), sems(8), sems(4, 4), sems(4, 4), sems(2, 4), sems(2, 4),
            sems(2, 4), sems(2, 4), sems(8), sems(8),
        ],
        compiler_params=pltpu.CompilerParams(collective_id=1, has_side_effects=True, vmem_limit_bytes=VMEM_LIMIT),
        name="scatter",
    )(dq, part)
    return (
        gq.reshape(SLICE, 32, HD),
        gk.reshape(SLICE, HEADS, HD),
        gv.reshape(SLICE, HEADS, HD),
    )


def solution(mesh):
    placed = P(("tok", "head"), None, None)
    return jax.shard_map(
        local,
        mesh=mesh,
        in_specs=(placed, placed, placed, placed, P()),
        out_specs=(placed, placed, placed),
        check_vma=False,
    )
```

```python
import math

import jax
import jax.numpy as jnp
from jax import lax
from jax.experimental import pallas as pl
from jax.experimental.pallas import tpu as pltpu
from jax.sharding import PartitionSpec as P

BLK = 128
HD = 128
GROUP = 4
HEADS = 8
NX, NY, NC = 4, 4, 2
NT = NX * NY * NC
SLICE = 32
DEPTH = 16
SLOTS = DEPTH + 1
ZERO_SLOT = SLOTS
POOL = NT + 1
ROWS = BLK * GROUP
KEYS = SLOTS * BLK
FACTOR = 1.0 / math.sqrt(HD)
SCALE2 = FACTOR * math.log2(math.e)
HIDDEN = -1e30
GS = 4
Z_ORDER = (4, 3, 5, 2, 6, 1, 7)
AROUND = sorted(((d, e) for d in range(NX) for e in range(NY) if d or e), key=lambda o: -sum(min(n, 4 - n) for n in o))
VMEM_LIMIT = 56 * 1024 * 1024
MESH = pl.DeviceIdType.MESH


def remote(src, dst, send_sem, recv_sem, **where):
    return pltpu.make_async_remote_copy(
        src_ref=src,
        dst_ref=dst,
        send_sem=send_sem,
        recv_sem=recv_sem,
        device_id=where,
        device_id_type=MESH,
    )


def tok_at(x, y, c):
    return (x % NX) * (NY * NC) + (y % NY) * NC + c


def one_hot(source):
    rows = lax.broadcasted_iota(jnp.int32, (256, 256), 0)
    cols = lax.broadcasted_iota(jnp.int32, (256, 256), 1)
    return jnp.where(source(rows) == cols, 1.0, 0.0).astype(jnp.bfloat16)


def exact_dot(picks, rows):
    return jnp.dot(picks, rows, preferred_element_type=jnp.float32).astype(jnp.bfloat16)


def regroup(i):
    return (i // 4 % 8) * 32 + (i // 32) * 4 + i % 4


def kv_heads_first(i):
    return (i % 32) * 8 + i // 32


def kv_tokens_first(i):
    return (i % 8) * 32 + i // 8


def fold(tile, op):
    return op(tile.reshape(-1, 8, ROWS), axis=0)


def f32_dot(a, b):
    return jnp.dot(a, b, preferred_element_type=jnp.float32)


def kernel(
    anc_hbm, q_hbm, k_hbm, v_hbm, g_hbm,
    gq_ref, gk_ref, gv_ref,
    anc, q_raw, k_raw, v_raw, g_raw, load_sem,
    ks, vs, qs, gs, q_in, g_in, kpool, vpool,
    chain, inverse, score0, score1, dprob0, dprob1, dscore0, dscore1, parts,
    dvpool, dkpool, core_in, plane, rs_in, home, home_in, dqs, dq_in,
    in_send, in_recv, pool_send, pool_recv, share_send, share_recv,
    half_send, half_recv, rs_send, rs_recv, home_send, home_recv, dq_send, dq_recv,
):
    t = lax.axis_index("tok")
    z = lax.axis_index("head")
    x, y, c = t // (NY * NC), (t // NC) % NY, t % NC
    sibling = tok_at(x, y, 1 - c)
    sent = []

    def launch(copy):
        copy.start()
        sent.append(copy)
        return copy

    loads = []
    for i, (src, dst) in enumerate(((k_hbm, k_raw), (v_hbm, v_raw), (q_hbm, q_raw), (g_hbm, g_raw), (anc_hbm, anc))):
        load = pltpu.make_async_copy(src, dst, load_sem.at[i])
        load.start()
        loads.append(load)
    barrier = pltpu.get_barrier_semaphore()
    for dz in range(1, HEADS):
        pl.semaphore_signal(barrier, inc=1, device_id={"head": (z + dz) % HEADS}, device_id_type=MESH)
    for d, e in AROUND:
        pl.semaphore_signal(barrier, inc=1, device_id={"tok": tok_at(x + d, y + e, c)}, device_id_type=MESH)
    pl.semaphore_signal(barrier, inc=1, device_id={"tok": sibling}, device_id_type=MESH)

    picks = one_hot(kv_heads_first)
    slot = jnp.where(z < 4, t, NT)
    rows = pl.ds(pl.multiple_of((z % 4) * SLICE, SLICE), SLICE)
    for i, (raw, out, pool) in enumerate(((k_raw, ks, kpool), (v_raw, vs, vpool))):
        loads[i].wait()
        out[...] = exact_dot(picks, raw[...]).reshape(HEADS, SLICE, HD)
        pool[slot, rows, :] = out[z]
    picks = one_hot(regroup)

    def group_heads(i, raw, out, into):
        loads[i].wait()
        for o in range(4):
            moved = exact_dot(picks, raw[o * 256 : (o + 1) * 256, :])
            out[:, o * 32 : (o + 1) * 32, :] = moved.reshape(HEADS, 32, HD)
        into[z] = out[z]

    group_heads(2, q_raw, qs, q_in)
    group_heads(3, g_raw, gs, g_in)
    pl.semaphore_wait(barrier, HEADS - 1 + len(AROUND) + 1)

    arrivals = [[], [], [], []]
    for i, (src, pool) in enumerate(((ks, kpool), (vs, vpool))):
        for dz in Z_ORDER:
            to = (z + dz) % HEADS
            copy = remote(src.at[to], pool.at[slot, rows, :], in_send.at[i, dz], in_recv.at[i, dz], head=to)
            arrivals[i].append(launch(copy))
    for i, (src, into) in ((2, (qs, q_in)), (3, (gs, g_in))):
        for dz in Z_ORDER:
            to = (z + dz) % HEADS
            copy = remote(src.at[to], into.at[z], in_send.at[i, dz], in_recv.at[i, dz], head=to)
            arrivals[i].append(launch(copy))

    loads[4].wait()
    for b in range(2):
        chain[b, 0] = t if b == 0 else jnp.int32(NT)
        for s in range(DEPTH):
            a = anc[2 * t + b, s]
            chain[b, 1 + s] = jnp.where(a < 0, -1, jnp.where(a % 2 == 1, NT, a // 2))

    @pl.loop(0, POOL)
    def _(p):
        for b in range(2):
            at = jnp.int32(ZERO_SLOT)
            for s in range(SLOTS):
                at = jnp.where(chain[b, s] == p, s, at)
            inverse[b, p] = at

    parts[:, ZERO_SLOT] = jnp.zeros((2, BLK, HD), jnp.float32)

    pools = (kpool, vpool)

    def pool_copy(i, d, e):
        ref = pools[i].at[t]
        return remote(ref, ref, pool_send.at[i, d, e], pool_recv.at[i, d, e], tok=tok_at(x + d, y + e, c))

    def share(i, d, e):
        ref = pools[i].at[tok_at(x - d, y - e, c)]
        return remote(ref, ref, share_send.at[i, d, e], share_recv.at[i, d, e], tok=sibling)

    def await_pool(i, d, e):
        ref = pools[i].at[tok_at(x - d, y - e, c)]
        remote(ref, ref, pool_send.at[i, d, e], pool_recv.at[i, d, e], tok=t).wait_recv()

    def await_share(i, d, e):
        ref = pools[i].at[tok_at(x - d, y - e, 1 - c)]
        remote(ref, ref, share_send.at[i, d, e], share_recv.at[i, d, e], tok=t).wait_recv()

    def forward(i, offsets):
        for d, e in offsets:
            await_pool(i, d, e)
            launch(share(i, d, e))

    for copy in arrivals[0]:
        copy.wait_recv()
    for d, e in AROUND:
        launch(pool_copy(0, d, e))
    launch(share(0, 0, 0))
    for copy in arrivals[1]:
        copy.wait_recv()
    forward(0, AROUND[:6])
    for d, e in AROUND:
        launch(pool_copy(1, d, e))
    launch(share(1, 0, 0))
    forward(0, AROUND[6:])
    for copy in arrivals[2] + arrivals[3]:
        copy.wait_recv()
    q = [q_in[4 * b : 4 * b + 4].reshape(ROWS, HD) for b in range(2)]
    g = [g_in[4 * b : 4 * b + 4].reshape(ROWS, HD) for b in range(2)]
    qt = [tile.T for tile in q]
    gt = [tile.T for tile in g]
    for d, e in [(0, 0)] + AROUND:
        await_share(0, d, e)

    score, dprob, dscore = (score0, score1), (dprob0, dprob1), (dscore0, dscore1)

    def tiles(pool, b, first, count):
        found = [pool[jnp.maximum(chain[b, first + j], 0)] for j in range(count)]
        return found[0] if count == 1 else jnp.concatenate(found, axis=0)

    def rows_of(first, count):
        return pl.ds(first * BLK, count * BLK)

    def sweep(step, state):
        state = step(0, 1, state)
        return lax.fori_loop(0, DEPTH // GS, lambda n, state: step(1 + n * GS, GS, state), state)

    def beside(one, two):
        return lambda first, count, state: (one(first, count, state[0]), two(first, count, state[1]))

    def look(b):
        def step(first, count, top):
            s = f32_dot(tiles(kpool, b, first, count), qt[b])
            for j in range(count):
                part = s[j * BLK : (j + 1) * BLK]
                if count == 1:
                    key = lax.broadcasted_iota(jnp.int32, (BLK, ROWS), 0)
                    row = lax.broadcasted_iota(jnp.int32, (BLK, ROWS), 1)
                    part = jnp.where(key * GROUP <= row, part, HIDDEN)
                else:
                    part = part + jnp.where(chain[b, first + j] >= 0, 0.0, HIDDEN)
                score[b][rows_of(first + j, 1), :] = part
                top = jnp.maximum(top, fold(part, jnp.max))
            return top

        return step

    def top_of(top):
        return jnp.max(top, axis=0, keepdims=True) * SCALE2

    def soften(b, top):
        def step(first, count, total):
            e = jnp.exp2(score[b][rows_of(first, count), :] * SCALE2 - top)
            score[b][rows_of(first, count), :] = e
            return total + fold(e, jnp.sum)

        return step

    def over_of(total):
        return 1.0 / jnp.sum(total, axis=0, keepdims=True)

    def value_part(b, over):
        def step(first, count, state):
            p = score[b][rows_of(first, count), :] * over
            dv = f32_dot(p.astype(jnp.bfloat16), g[b])
            for j in range(count):
                parts[b, first + j] = dv[j * BLK : (j + 1) * BLK]
            return state

        return step

    def cross(b):
        def step(first, count, weighted):
            dp = f32_dot(tiles(vpool, b, first, count), gt[b])
            dprob[b][rows_of(first, count), :] = dp
            return weighted + fold(score[b][rows_of(first, count), :] * dp, jnp.sum)

        return step

    def key_part(b, over, delta):
        def step(first, count, state):
            p = score[b][rows_of(first, count), :] * over
            ds = (p * (dprob[b][rows_of(first, count), :] - delta)).astype(jnp.bfloat16)
            dscore[b][rows_of(first, count), :] = ds
            dk = f32_dot(ds, q[b]) * FACTOR
            for j in range(count):
                parts[b, first + j] = dk[j * BLK : (j + 1) * BLK]
            return state

        return step

    def query_part(b):
        def step(first, count, dqt):
            return dqt + lax.dot_general(
                tiles(kpool, b, first, count), dscore[b][rows_of(first, count), :],
                (((0,), (0,)), ((), ())), preferred_element_type=jnp.float32,
            )

        return step

    halves = (dkpool, dvpool)

    def total_of(p):
        return parts[0, inverse[0, p]] + parts[1, inverse[1, p]]

    def half_copy(i, d, e):
        return remote(
            halves[i].at[d * NY + e], core_in.at[i, d, e], half_send.at[i, d, e], half_recv.at[i, d, e], tok=sibling
        )

    def rs_copy(i, d, e):
        return remote(
            plane.at[i, d, e], rs_in.at[i, d, e], rs_send.at[i, d, e], rs_recv.at[i, d, e], tok=tok_at(x + d, y + e, c)
        )

    def give_halves(i):
        for d, e in AROUND + [(0, 0)]:
            halves[i][d * NY + e] = total_of(tok_at(x + d, y + e, 1 - c)).astype(jnp.bfloat16)
            launch(half_copy(i, d, e))

    def give_homes(i):
        for d, e in AROUND:
            mine = total_of(tok_at(x + d, y + e, c))
            half_copy(i, d, e).wait_recv()
            plane[i, d, e] = (mine + core_in[i, d, e].astype(jnp.float32)).astype(jnp.bfloat16)
            launch(rs_copy(i, d, e))
        mine = total_of(t)
        half_copy(i, 0, 0).wait_recv()
        home[i, 4:8] = total_of(NT).astype(jnp.bfloat16).reshape(4, SLICE, HD)
        return mine + core_in[i, 0, 0].astype(jnp.float32)

    def to_tokens(i, total):
        for d, e in AROUND:
            rs_copy(i, d, e).wait_recv()
            total = total + rs_in[i, d, e].astype(jnp.float32)
        home[i, 0:4] = total.astype(jnp.bfloat16).reshape(4, SLICE, HD)
        copies = []
        for dz in Z_ORDER:
            to = (z + dz) % HEADS
            copies.append(launch(remote(home.at[i, to], home_in.at[i, z], home_send.at[i, dz], home_recv.at[i, dz], head=to)))
        home_in[i, z] = home[i, z]
        return copies

    start = jnp.full((8, ROWS), HIDDEN, jnp.float32)
    zero = jnp.zeros((8, ROWS), jnp.float32)
    none = jnp.int32(0)
    top0 = top_of(sweep(look(0), start))
    total0, top1 = sweep(beside(soften(0, top0), look(1)), (zero, start))
    over0, top1 = over_of(total0), top_of(top1)
    forward(1, AROUND[:5])
    _, total1 = sweep(beside(value_part(0, over0), soften(1, top1)), (none, zero))
    over1 = over_of(total1)
    forward(1, AROUND[5:10])
    sweep(value_part(1, over1), none)
    forward(1, AROUND[10:])
    give_halves(1)
    for d, e in [(0, 0)] + AROUND:
        await_share(1, d, e)
    weighted0 = sweep(cross(0), zero)
    mine_v = give_homes(1)
    delta0 = jnp.sum(weighted0, axis=0, keepdims=True) * over0
    _, weighted1 = sweep(beside(key_part(0, over0, delta0), cross(1)), (none, zero))
    delta1 = jnp.sum(weighted1, axis=0, keepdims=True) * over1
    sweep(key_part(1, over1, delta1), none)
    give_halves(0)

    empty = jnp.zeros((HD, ROWS), jnp.float32)
    dqt = sweep(beside(query_part(0), query_part(1)), (empty, empty))
    for b in range(2):
        dqs[4 * b : 4 * b + 4] = (dqt[b] * FACTOR).T.astype(jnp.bfloat16).reshape(4, SLICE * GROUP, HD)
    mine_k = give_homes(0)
    dq_copies = []
    for dz in Z_ORDER:
        to = (z + dz) % HEADS
        dq_copies.append(launch(remote(dqs.at[to], dq_in.at[z], dq_send.at[dz], dq_recv.at[dz], head=to)))
    dq_in[z] = dqs[z]
    v_copies = to_tokens(1, mine_v)

    picks = one_hot(regroup)
    for copy in dq_copies:
        copy.wait_recv()
    for o in range(4):
        moved = dq_in[:, o * 32 : (o + 1) * 32, :].reshape(256, HD)
        gq_ref[o * 256 : (o + 1) * 256, :] = exact_dot(picks, moved)
    picks = one_hot(kv_tokens_first)
    for copy in v_copies:
        copy.wait_recv()
    gv_ref[...] = exact_dot(picks, home_in[1].reshape(256, HD))
    for copy in to_tokens(0, mine_k):
        copy.wait_recv()
    gk_ref[...] = exact_dot(picks, home_in[0].reshape(256, HD))
    for copy in sent:
        copy.wait_send()


def store_kernel(gq, gk, gv, gq_out, gk_out, gv_out, sem):
    copies = [
        pltpu.make_async_copy(src, dst, sem.at[i])
        for i, (src, dst) in enumerate(((gq, gq_out), (gk, gk_out), (gv, gv_out)))
    ]
    for copy in copies:
        copy.start()
    for copy in copies:
        copy.wait()


def whole():
    return pl.BlockSpec(memory_space=pltpu.VMEM)


def anywhere():
    return pl.BlockSpec(memory_space=pl.ANY)


def shape(*dims):
    return jax.ShapeDtypeStruct(dims, jnp.bfloat16)


def buffer(*dims, dtype=jnp.bfloat16):
    return pltpu.VMEM(dims, dtype)


def sems(*dims):
    return pltpu.SemaphoreType.DMA(dims)


def local(queries, keys, values, grad_out, ancestry):
    rows = SLICE * GROUP
    results = (shape(SLICE * 32, HD), shape(SLICE * HEADS, HD), shape(SLICE * HEADS, HD))
    grads = pl.pallas_call(
        kernel,
        out_shape=results,
        in_specs=[anywhere()] * 5,
        out_specs=(whole(),) * 3,
        scratch_shapes=[
            pltpu.SMEM(ancestry.shape, jnp.int32),
            buffer(SLICE * 32, HD), buffer(SLICE * HEADS, HD), buffer(SLICE * HEADS, HD), buffer(SLICE * 32, HD),
            sems(5),
            buffer(HEADS, SLICE, HD), buffer(HEADS, SLICE, HD), buffer(HEADS, rows, HD), buffer(HEADS, rows, HD),
            buffer(HEADS, rows, HD), buffer(HEADS, rows, HD), buffer(POOL, BLK, HD), buffer(POOL, BLK, HD),
            pltpu.SMEM((2, SLOTS), jnp.int32), pltpu.SMEM((2, POOL), jnp.int32),
            buffer(KEYS, ROWS, dtype=jnp.float32), buffer(KEYS, ROWS, dtype=jnp.float32),
            buffer(KEYS, ROWS, dtype=jnp.float32), buffer(KEYS, ROWS, dtype=jnp.float32),
            buffer(KEYS, ROWS), buffer(KEYS, ROWS),
            buffer(2, SLOTS + 1, BLK, HD, dtype=jnp.float32),
            buffer(NX * NY, BLK, HD), buffer(NX * NY, BLK, HD),
            buffer(2, NX, NY, BLK, HD), buffer(2, NX, NY, BLK, HD), buffer(2, NX, NY, BLK, HD),
            buffer(2, HEADS, SLICE, HD), buffer(2, HEADS, SLICE, HD), buffer(HEADS, rows, HD), buffer(HEADS, rows, HD),
            sems(4, 8), sems(4, 8), sems(2, 4, 4), sems(2, 4, 4), sems(2, 4, 4), sems(2, 4, 4),
            sems(2, 4, 4), sems(2, 4, 4), sems(2, 4, 4), sems(2, 4, 4), sems(2, 8), sems(2, 8), sems(8), sems(8),
        ],
        compiler_params=pltpu.CompilerParams(collective_id=0, has_side_effects=True, vmem_limit_bytes=VMEM_LIMIT),
        name="backward",
    )(
        ancestry,
        queries.reshape(SLICE * 32, HD),
        keys.reshape(SLICE * HEADS, HD),
        values.reshape(SLICE * HEADS, HD),
        grad_out.reshape(SLICE * 32, HD),
    )
    gq, gk, gv = pl.pallas_call(
        store_kernel,
        out_shape=results,
        in_specs=[whole()] * 3,
        out_specs=(anywhere(),) * 3,
        scratch_shapes=[sems(3)],
        name="store",
    )(*grads)
    return (
        gq.reshape(SLICE, 32, HD),
        gk.reshape(SLICE, HEADS, HD),
        gv.reshape(SLICE, HEADS, HD),
    )


def solution(mesh):
    placed = P(("tok", "head"), None, None)
    return jax.shard_map(
        local,
        mesh=mesh,
        in_specs=(placed, placed, placed, placed, P()),
        out_specs=(placed, placed, placed),
        check_vma=False,
    )
```

```python
import math

import jax
import jax.numpy as jnp
from jax import lax
from jax.experimental import pallas as pl
from jax.experimental.pallas import tpu as pltpu
from jax.sharding import PartitionSpec as P

BLK = 128
HD = 128
GROUP = 4
HEADS = 8
NX, NY, NC = 4, 4, 2
NT = NX * NY * NC
SLICE = 32
DEPTH = 16
SLOTS = DEPTH + 1
ZERO_SLOT = SLOTS
POOL = NT + 1
ROWS = BLK * GROUP
KEYS = SLOTS * BLK
FACTOR = 1.0 / math.sqrt(HD)
SCALE2 = FACTOR * math.log2(math.e)
HIDDEN = -1e30
GS = 8
Z_ORDER = (4, 3, 5, 2, 6, 1, 7)
AROUND = sorted(((d, e) for d in range(NX) for e in range(NY) if d or e), key=lambda o: -sum(min(n, 4 - n) for n in o))
VMEM_LIMIT = 56 * 1024 * 1024
MESH = pl.DeviceIdType.MESH


def remote(src, dst, send_sem, recv_sem, **where):
    return pltpu.make_async_remote_copy(
        src_ref=src,
        dst_ref=dst,
        send_sem=send_sem,
        recv_sem=recv_sem,
        device_id=where,
        device_id_type=MESH,
    )


def tok_at(x, y, c):
    return (x % NX) * (NY * NC) + (y % NY) * NC + c


def one_hot(source):
    rows = lax.broadcasted_iota(jnp.int32, (256, 256), 0)
    cols = lax.broadcasted_iota(jnp.int32, (256, 256), 1)
    return jnp.where(source(rows) == cols, 1.0, 0.0).astype(jnp.bfloat16)


def exact_dot(picks, rows):
    return jnp.dot(picks, rows, preferred_element_type=jnp.float32).astype(jnp.bfloat16)


def regroup(i):
    return (i // 4 % 8) * 32 + (i // 32) * 4 + i % 4


def kv_heads_first(i):
    return (i % 32) * 8 + i // 32


def kv_tokens_first(i):
    return (i % 8) * 32 + i // 8


def fold(tile, op):
    return op(tile.reshape(-1, 8, ROWS), axis=0)


def f32_dot(a, b):
    return jnp.dot(a, b, preferred_element_type=jnp.float32)


def kernel(
    anc_hbm, q_hbm, k_hbm, v_hbm, g_hbm,
    gq_ref, gk_ref, gv_ref,
    anc, q_raw, k_raw, v_raw, g_raw, load_sem,
    ks, vs, qs, gs, q_in, g_in, kpool, vpool,
    chain, inverse, score0, score1, dprob0, dprob1, dscore0, dscore1, parts,
    dvpool, dkpool, core_in, plane, rs_in, home, home_in, dqs, dq_in,
    in_send, in_recv, pool_send, pool_recv, share_send, share_recv,
    half_send, half_recv, rs_send, rs_recv, home_send, home_recv, dq_send, dq_recv,
):
    t = lax.axis_index("tok")
    z = lax.axis_index("head")
    x, y, c = t // (NY * NC), (t // NC) % NY, t % NC
    sibling = tok_at(x, y, 1 - c)
    sent = []

    def launch(copy):
        copy.start()
        sent.append(copy)
        return copy

    def settle():
        while sent:
            sent.pop(0).wait_send()

    loads = []
    for i, (src, dst) in enumerate(((k_hbm, k_raw), (v_hbm, v_raw), (q_hbm, q_raw), (g_hbm, g_raw), (anc_hbm, anc))):
        load = pltpu.make_async_copy(src, dst, load_sem.at[i])
        load.start()
        loads.append(load)
    barrier = pltpu.get_barrier_semaphore()
    for dz in range(1, HEADS):
        pl.semaphore_signal(barrier, inc=1, device_id={"head": (z + dz) % HEADS}, device_id_type=MESH)
    for d, e in AROUND:
        pl.semaphore_signal(barrier, inc=1, device_id={"tok": tok_at(x + d, y + e, c)}, device_id_type=MESH)
    pl.semaphore_signal(barrier, inc=1, device_id={"tok": sibling}, device_id_type=MESH)

    slot = jnp.where(z < 4, t, NT)
    rows = pl.ds(pl.multiple_of((z % 4) * SLICE, SLICE), SLICE)
    arrivals = [[], [], [], []]

    def send_kv(i, src, pool):
        for dz in Z_ORDER:
            to = (z + dz) % HEADS
            copy = remote(src.at[to], pool.at[slot, rows, :], in_send.at[i, dz], in_recv.at[i, dz], head=to)
            arrivals[i].append(launch(copy))

    def send_heads(i, src, into):
        for dz in Z_ORDER:
            to = (z + dz) % HEADS
            copy = remote(src.at[to], into.at[z], in_send.at[i, dz], in_recv.at[i, dz], head=to)
            arrivals[i].append(launch(copy))

    def group_kv(i, raw, out, pool):
        loads[i].wait()
        out[...] = exact_dot(kv_picks, raw[...]).reshape(HEADS, SLICE, HD)
        pool[slot, rows, :] = out[z]

    def group_heads(i, raw, out, into):
        loads[i].wait()
        for o in range(4):
            moved = exact_dot(picks, raw[o * 256 : (o + 1) * 256, :])
            out[:, o * 32 : (o + 1) * 32, :] = moved.reshape(HEADS, 32, HD)
        into[z] = out[z]

    kv_picks = one_hot(kv_heads_first)
    group_kv(0, k_raw, ks, kpool)
    pl.semaphore_wait(barrier, HEADS - 1 + len(AROUND) + 1)
    send_kv(0, ks, kpool)
    group_kv(1, v_raw, vs, vpool)
    send_kv(1, vs, vpool)
    picks = one_hot(regroup)
    group_heads(2, q_raw, qs, q_in)
    send_heads(2, qs, q_in)
    group_heads(3, g_raw, gs, g_in)
    send_heads(3, gs, g_in)

    loads[4].wait()
    for b in range(2):
        chain[b, 0] = t if b == 0 else jnp.int32(NT)
        for s in range(DEPTH):
            a = anc[s, 2 * t + b]
            chain[b, 1 + s] = jnp.where(a < 0, -1, jnp.where(a % 2 == 1, NT, a // 2))

    @pl.loop(0, POOL)
    def _(p):
        for b in range(2):
            at = jnp.int32(ZERO_SLOT)
            for s in range(SLOTS):
                at = jnp.where(chain[b, s] == p, s, at)
            inverse[b, p] = at

    parts[:, ZERO_SLOT] = jnp.zeros((2, BLK, HD), jnp.float32)

    pools = (kpool, vpool)

    def pool_copy(i, d, e):
        ref = pools[i].at[t]
        return remote(ref, ref, pool_send.at[i, d, e], pool_recv.at[i, d, e], tok=tok_at(x + d, y + e, c))

    def share(i, d, e):
        ref = pools[i].at[tok_at(x - d, y - e, c)]
        return remote(ref, ref, share_send.at[i, d, e], share_recv.at[i, d, e], tok=sibling)

    def await_pool(i, d, e):
        ref = pools[i].at[tok_at(x - d, y - e, c)]
        remote(ref, ref, pool_send.at[i, d, e], pool_recv.at[i, d, e], tok=t).wait_recv()

    def await_share(i, d, e):
        ref = pools[i].at[tok_at(x - d, y - e, 1 - c)]
        remote(ref, ref, share_send.at[i, d, e], share_recv.at[i, d, e], tok=t).wait_recv()

    def forward(i, offsets):
        for d, e in offsets:
            await_pool(i, d, e)
            launch(share(i, d, e))

    for copy in arrivals[0]:
        copy.wait_recv()
    for d, e in AROUND:
        launch(pool_copy(0, d, e))
    launch(share(0, 0, 0))
    for copy in arrivals[1]:
        copy.wait_recv()
    forward(0, AROUND[:6])
    for d, e in AROUND:
        launch(pool_copy(1, d, e))
    launch(share(1, 0, 0))
    forward(0, AROUND[6:])
    for copy in arrivals[2]:
        copy.wait_recv()
    q = [q_in[4 * b : 4 * b + 4].reshape(ROWS, HD) for b in range(2)]
    qt = [tile.T for tile in q]
    for d, e in [(0, 0)] + AROUND:
        await_share(0, d, e)

    score, dprob, dscore = (score0, score1), (dprob0, dprob1), (dscore0, dscore1)

    def tiles(pool, b, first, count):
        found = [pool[jnp.maximum(chain[b, first + j], 0)] for j in range(count)]
        return found[0] if count == 1 else jnp.concatenate(found, axis=0)

    def rows_of(first, count):
        return pl.ds(first * BLK, count * BLK)

    def sweep(step, state):
        state = step(0, 1, state)
        return lax.fori_loop(0, DEPTH // GS, lambda n, state: step(1 + n * GS, GS, state), state)

    def beside(one, two):
        return lambda first, count, state: (one(first, count, state[0]), two(first, count, state[1]))

    def look(b):
        def step(first, count, top):
            s = f32_dot(tiles(kpool, b, first, count), qt[b])
            for j in range(count):
                part = s[j * BLK : (j + 1) * BLK]
                if count == 1:
                    key = lax.broadcasted_iota(jnp.int32, (BLK, ROWS), 0)
                    row = lax.broadcasted_iota(jnp.int32, (BLK, ROWS), 1)
                    part = jnp.where(key * GROUP <= row, part, HIDDEN)
                else:
                    part = part + jnp.where(chain[b, first + j] >= 0, 0.0, HIDDEN)
                score[b][rows_of(first + j, 1), :] = part
                top = jnp.maximum(top, fold(part, jnp.max))
            return top

        return step

    def top_of(top):
        return jnp.max(top, axis=0, keepdims=True) * SCALE2

    def soften(b, top):
        def step(first, count, total):
            e = jnp.exp2(score[b][rows_of(first, count), :] * SCALE2 - top)
            score[b][rows_of(first, count), :] = e
            return total + fold(e, jnp.sum)

        return step

    def over_of(total):
        return 1.0 / jnp.sum(total, axis=0, keepdims=True)

    def value_part(b, over):
        def step(first, count, state):
            p = score[b][rows_of(first, count), :] * over
            dv = f32_dot(p.astype(jnp.bfloat16), g[b])
            for j in range(count):
                parts[b, first + j] = dv[j * BLK : (j + 1) * BLK]
            return state

        return step

    def cross(b):
        def step(first, count, weighted):
            dp = f32_dot(tiles(vpool, b, first, count), gt[b])
            dprob[b][rows_of(first, count), :] = dp
            return weighted + fold(score[b][rows_of(first, count), :] * dp, jnp.sum)

        return step

    def key_part(b, over, delta):
        def step(first, count, state):
            p = score[b][rows_of(first, count), :] * over
            ds = (p * (dprob[b][rows_of(first, count), :] - delta)).astype(jnp.bfloat16)
            dscore[b][rows_of(first, count), :] = ds
            dk = f32_dot(ds, q[b]) * FACTOR
            for j in range(count):
                parts[b, first + j] = dk[j * BLK : (j + 1) * BLK]
            return state

        return step

    def query_part(b):
        def step(first, count, dqt):
            return dqt + lax.dot_general(
                tiles(kpool, b, first, count), dscore[b][rows_of(first, count), :],
                (((0,), (0,)), ((), ())), preferred_element_type=jnp.float32,
            )

        return step

    halves = (dkpool, dvpool)

    def total_of(p):
        return parts[0, inverse[0, p]] + parts[1, inverse[1, p]]

    def half_copy(i, d, e):
        return remote(
            halves[i].at[d * NY + e], core_in.at[i, d, e], half_send.at[i, d, e], half_recv.at[i, d, e], tok=sibling
        )

    def rs_copy(i, d, e):
        return remote(
            plane.at[i, d, e], rs_in.at[i, d, e], rs_send.at[i, d, e], rs_recv.at[i, d, e], tok=tok_at(x + d, y + e, c)
        )

    def give_halves(i):
        for d, e in AROUND + [(0, 0)]:
            halves[i][d * NY + e] = total_of(tok_at(x + d, y + e, 1 - c)).astype(jnp.bfloat16)
            launch(half_copy(i, d, e))

    def give_homes(i):
        for d, e in AROUND:
            mine = total_of(tok_at(x + d, y + e, c))
            half_copy(i, d, e).wait_recv()
            plane[i, d, e] = (mine + core_in[i, d, e].astype(jnp.float32)).astype(jnp.bfloat16)
            launch(rs_copy(i, d, e))
        mine = total_of(t)
        half_copy(i, 0, 0).wait_recv()
        home[i, 4:8] = total_of(NT).astype(jnp.bfloat16).reshape(4, SLICE, HD)
        return mine + core_in[i, 0, 0].astype(jnp.float32)

    def to_tokens(i, total):
        for d, e in AROUND:
            rs_copy(i, d, e).wait_recv()
            total = total + rs_in[i, d, e].astype(jnp.float32)
        home[i, 0:4] = total.astype(jnp.bfloat16).reshape(4, SLICE, HD)
        copies = []
        for dz in Z_ORDER:
            to = (z + dz) % HEADS
            copies.append(launch(remote(home.at[i, to], home_in.at[i, z], home_send.at[i, dz], home_recv.at[i, dz], head=to)))
        home_in[i, z] = home[i, z]
        return copies

    start = jnp.full((8, ROWS), HIDDEN, jnp.float32)
    zero = jnp.zeros((8, ROWS), jnp.float32)
    none = jnp.int32(0)
    top0 = top_of(sweep(look(0), start))
    total0, top1 = sweep(beside(soften(0, top0), look(1)), (zero, start))
    over0, top1 = over_of(total0), top_of(top1)
    forward(1, AROUND[:5])
    total1 = sweep(soften(1, top1), zero)
    over1 = over_of(total1)
    for copy in arrivals[3]:
        copy.wait_recv()
    g = [g_in[4 * b : 4 * b + 4].reshape(ROWS, HD) for b in range(2)]
    gt = [tile.T for tile in g]
    forward(1, AROUND[5:10])
    sweep(beside(value_part(0, over0), value_part(1, over1)), (none, none))
    forward(1, AROUND[10:])
    give_halves(1)
    for d, e in [(0, 0)] + AROUND:
        await_share(1, d, e)
    weighted0 = sweep(cross(0), zero)
    mine_v = give_homes(1)
    delta0 = jnp.sum(weighted0, axis=0, keepdims=True) * over0
    _, weighted1 = sweep(beside(key_part(0, over0, delta0), cross(1)), (none, zero))
    delta1 = jnp.sum(weighted1, axis=0, keepdims=True) * over1
    sweep(key_part(1, over1, delta1), none)
    give_halves(0)

    empty = jnp.zeros((HD, ROWS), jnp.float32)
    dqt = sweep(beside(query_part(0), query_part(1)), (empty, empty))
    for b in range(2):
        dqs[4 * b : 4 * b + 4] = (dqt[b] * FACTOR).T.astype(jnp.bfloat16).reshape(4, SLICE * GROUP, HD)
    mine_k = give_homes(0)
    dq_copies = []
    for dz in Z_ORDER:
        to = (z + dz) % HEADS
        dq_copies.append(launch(remote(dqs.at[to], dq_in.at[z], dq_send.at[dz], dq_recv.at[dz], head=to)))
    dq_in[z] = dqs[z]
    v_copies = to_tokens(1, mine_v)

    settle()
    picks = one_hot(regroup)
    for copy in dq_copies:
        copy.wait_recv()
    for o in range(4):
        moved = dq_in[:, o * 32 : (o + 1) * 32, :].reshape(256, HD)
        gq_ref[o * 256 : (o + 1) * 256, :] = exact_dot(picks, moved)
    picks = one_hot(kv_tokens_first)
    for copy in v_copies:
        copy.wait_recv()
    gv_ref[...] = exact_dot(picks, home_in[1].reshape(256, HD))
    for copy in to_tokens(0, mine_k):
        copy.wait_recv()
    gk_ref[...] = exact_dot(picks, home_in[0].reshape(256, HD))
    settle()


def store_kernel(gq, gk, gv, gq_out, gk_out, gv_out, sem):
    copies = [
        pltpu.make_async_copy(src, dst, sem.at[i])
        for i, (src, dst) in enumerate(((gq, gq_out), (gk, gk_out), (gv, gv_out)))
    ]
    for copy in copies:
        copy.start()
    for copy in copies:
        copy.wait()


def whole():
    return pl.BlockSpec(memory_space=pltpu.VMEM)


def anywhere():
    return pl.BlockSpec(memory_space=pl.ANY)


def shape(*dims):
    return jax.ShapeDtypeStruct(dims, jnp.bfloat16)


def buffer(*dims, dtype=jnp.bfloat16):
    return pltpu.VMEM(dims, dtype)


def sems(*dims):
    return pltpu.SemaphoreType.DMA(dims)


def local(queries, keys, values, grad_out, ancestry):
    rows = SLICE * GROUP
    results = (shape(SLICE * 32, HD), shape(SLICE * HEADS, HD), shape(SLICE * HEADS, HD))
    grads = pl.pallas_call(
        kernel,
        out_shape=tuple(pltpu.VMEM(r.shape, r.dtype) for r in results),
        in_specs=[anywhere()] * 5,
        out_specs=(whole(),) * 3,
        scratch_shapes=[
            pltpu.SMEM((DEPTH, 2 * NT), jnp.int32),
            buffer(SLICE * 32, HD), buffer(SLICE * HEADS, HD), buffer(SLICE * HEADS, HD), buffer(SLICE * 32, HD),
            sems(5),
            buffer(HEADS, SLICE, HD), buffer(HEADS, SLICE, HD), buffer(HEADS, rows, HD), buffer(HEADS, rows, HD),
            buffer(HEADS, rows, HD), buffer(HEADS, rows, HD), buffer(POOL, BLK, HD), buffer(POOL, BLK, HD),
            pltpu.SMEM((2, SLOTS), jnp.int32), pltpu.SMEM((2, POOL), jnp.int32),
            buffer(KEYS, ROWS, dtype=jnp.float32), buffer(KEYS, ROWS, dtype=jnp.float32),
            buffer(KEYS, ROWS, dtype=jnp.float32), buffer(KEYS, ROWS, dtype=jnp.float32),
            buffer(KEYS, ROWS), buffer(KEYS, ROWS),
            buffer(2, SLOTS + 1, BLK, HD, dtype=jnp.float32),
            buffer(NX * NY, BLK, HD), buffer(NX * NY, BLK, HD),
            buffer(2, NX, NY, BLK, HD), buffer(2, NX, NY, BLK, HD), buffer(2, NX, NY, BLK, HD),
            buffer(2, HEADS, SLICE, HD), buffer(2, HEADS, SLICE, HD), buffer(HEADS, rows, HD), buffer(HEADS, rows, HD),
            sems(4, 8), sems(4, 8), sems(2, 4, 4), sems(2, 4, 4), sems(2, 4, 4), sems(2, 4, 4),
            sems(2, 4, 4), sems(2, 4, 4), sems(2, 4, 4), sems(2, 4, 4), sems(2, 8), sems(2, 8), sems(8), sems(8),
        ],
        compiler_params=pltpu.CompilerParams(collective_id=0, has_side_effects=True, vmem_limit_bytes=VMEM_LIMIT),
        name="backward",
    )(
        ancestry.T,
        queries.reshape(SLICE * 32, HD),
        keys.reshape(SLICE * HEADS, HD),
        values.reshape(SLICE * HEADS, HD),
        grad_out.reshape(SLICE * 32, HD),
    )
    gq, gk, gv = pl.pallas_call(
        store_kernel,
        out_shape=results,
        in_specs=[whole()] * 3,
        out_specs=(anywhere(),) * 3,
        scratch_shapes=[sems(3)],
        name="store",
    )(*(pltpu.with_memory_space_constraint(r, pltpu.VMEM) for r in grads))
    return (
        gq.reshape(SLICE, 32, HD),
        gk.reshape(SLICE, HEADS, HD),
        gv.reshape(SLICE, HEADS, HD),
    )


def solution(mesh):
    placed = P(("tok", "head"), None, None)
    return jax.shard_map(
        local,
        mesh=mesh,
        in_specs=(placed, placed, placed, placed, P()),
        out_specs=(placed, placed, placed),
        check_vma=False,
    )
```

```python
import math

import jax
import jax.numpy as jnp
from jax import lax
from jax.experimental import pallas as pl
from jax.experimental.pallas import tpu as pltpu
from jax.sharding import PartitionSpec as P

BLK = 128
HD = 128
GROUP = 4
HEADS = 8
NX, NY, NC = 4, 4, 2
NT = NX * NY * NC
SLICE = 32
DEPTH = 16
SLOTS = DEPTH + 1
ZERO_SLOT = SLOTS
POOL = NT + 1
ROWS = BLK * GROUP
KEYS = SLOTS * BLK
FACTOR = 1.0 / math.sqrt(HD)
SCALE2 = FACTOR * math.log2(math.e)
HIDDEN = -1e30
GS = 8
Z_ORDER = (4, 3, 5, 2, 6, 1, 7)
AROUND = sorted(((d, e) for d in range(NX) for e in range(NY) if d or e), key=lambda o: -sum(min(n, 4 - n) for n in o))
VMEM_LIMIT = 56 * 1024 * 1024
MESH = pl.DeviceIdType.MESH


def remote(src, dst, send_sem, recv_sem, **where):
    return pltpu.make_async_remote_copy(
        src_ref=src,
        dst_ref=dst,
        send_sem=send_sem,
        recv_sem=recv_sem,
        device_id=where,
        device_id_type=MESH,
    )


def tok_at(x, y, c):
    return (x % NX) * (NY * NC) + (y % NY) * NC + c


def one_hot(source):
    rows = lax.broadcasted_iota(jnp.int32, (256, 256), 0)
    cols = lax.broadcasted_iota(jnp.int32, (256, 256), 1)
    return jnp.where(source(rows) == cols, 1.0, 0.0).astype(jnp.bfloat16)


def exact_dot(picks, rows):
    return jnp.dot(picks, rows, preferred_element_type=jnp.float32).astype(jnp.bfloat16)


def regroup(i):
    return (i // 4 % 8) * 32 + (i // 32) * 4 + i % 4


def kv_heads_first(i):
    return (i % 32) * 8 + i // 32


def kv_tokens_first(i):
    return (i % 8) * 32 + i // 8


def fold(tile, op):
    return op(tile.reshape(-1, 8, ROWS), axis=0)


def f32_dot(a, b):
    return jnp.dot(a, b, preferred_element_type=jnp.float32)


def kernel(
    anc_hbm, q_hbm, k_hbm, v_hbm, g_hbm,
    gq_ref, gk_ref, gv_ref,
    anc, q_raw, k_raw, v_raw, g_raw, load_sem,
    ks, vs, qs, gs, q_in, g_in, kpool, vpool,
    chain, inverse, score0, score1, dprob0, dprob1, dscore0, dscore1, parts,
    dvpool, dkpool, core_in, plane, rs_in, home, home_in, dqs, dq_in,
    in_send, in_recv, pool_send, pool_recv, share_send, share_recv,
    half_send, half_recv, rs_send, rs_recv, home_send, home_recv, dq_send, dq_recv,
):
    t = lax.axis_index("tok")
    z = lax.axis_index("head")
    x, y, c = t // (NY * NC), (t // NC) % NY, t % NC
    sibling = tok_at(x, y, 1 - c)
    sent = []

    def launch(copy):
        copy.start()
        sent.append(copy)
        return copy

    def settle():
        while sent:
            sent.pop(0).wait_send()

    loads = []
    for i, (src, dst) in enumerate(((k_hbm, k_raw), (v_hbm, v_raw), (q_hbm, q_raw), (g_hbm, g_raw), (anc_hbm, anc))):
        load = pltpu.make_async_copy(src, dst, load_sem.at[i])
        load.start()
        loads.append(load)
    barrier = pltpu.get_barrier_semaphore()
    for dz in range(1, HEADS):
        pl.semaphore_signal(barrier, inc=1, device_id={"head": (z + dz) % HEADS}, device_id_type=MESH)
    for d, e in AROUND:
        pl.semaphore_signal(barrier, inc=1, device_id={"tok": tok_at(x + d, y + e, c)}, device_id_type=MESH)
    pl.semaphore_signal(barrier, inc=1, device_id={"tok": sibling}, device_id_type=MESH)

    slot = jnp.where(z < 4, t, NT)
    rows = pl.ds(pl.multiple_of((z % 4) * SLICE, SLICE), SLICE)
    arrivals = [[], [], [], []]

    def send_kv(i, src, pool):
        for dz in Z_ORDER:
            to = (z + dz) % HEADS
            copy = remote(src.at[to], pool.at[slot, rows, :], in_send.at[i, dz], in_recv.at[i, dz], head=to)
            arrivals[i].append(launch(copy))

    def send_heads(i, src, into):
        for dz in Z_ORDER:
            to = (z + dz) % HEADS
            copy = remote(src.at[to], into.at[z], in_send.at[i, dz], in_recv.at[i, dz], head=to)
            arrivals[i].append(launch(copy))

    def group_kv(i, raw, out, pool):
        loads[i].wait()
        out[...] = exact_dot(kv_picks, raw[...]).reshape(HEADS, SLICE, HD)
        pool[slot, rows, :] = out[z]

    def group_heads(i, raw, out, into):
        loads[i].wait()
        for o in range(4):
            moved = exact_dot(picks, raw[o * 256 : (o + 1) * 256, :])
            out[:, o * 32 : (o + 1) * 32, :] = moved.reshape(HEADS, 32, HD)
        into[z] = out[z]

    kv_picks = one_hot(kv_heads_first)
    group_kv(0, k_raw, ks, kpool)
    pl.semaphore_wait(barrier, HEADS - 1 + len(AROUND) + 1)
    send_kv(0, ks, kpool)
    group_kv(1, v_raw, vs, vpool)
    send_kv(1, vs, vpool)
    picks = one_hot(regroup)
    group_heads(2, q_raw, qs, q_in)
    send_heads(2, qs, q_in)
    group_heads(3, g_raw, gs, g_in)
    send_heads(3, gs, g_in)

    pools = (kpool, vpool)

    def pool_copy(i, d, e):
        ref = pools[i].at[t]
        return remote(ref, ref, pool_send.at[i, d, e], pool_recv.at[i, d, e], tok=tok_at(x + d, y + e, c))

    def share(i, d, e):
        ref = pools[i].at[tok_at(x - d, y - e, c)]
        return remote(ref, ref, share_send.at[i, d, e], share_recv.at[i, d, e], tok=sibling)

    def await_pool(i, d, e):
        ref = pools[i].at[tok_at(x - d, y - e, c)]
        remote(ref, ref, pool_send.at[i, d, e], pool_recv.at[i, d, e], tok=t).wait_recv()

    def await_share(i, d, e):
        ref = pools[i].at[tok_at(x - d, y - e, 1 - c)]
        remote(ref, ref, share_send.at[i, d, e], share_recv.at[i, d, e], tok=t).wait_recv()

    def forward(i, offsets):
        for d, e in offsets:
            await_pool(i, d, e)
            launch(share(i, d, e))

    for copy in arrivals[0]:
        copy.wait_recv()
    for d, e in AROUND:
        launch(pool_copy(0, d, e))
    launch(share(0, 0, 0))
    loads[4].wait()
    for b in range(2):
        chain[b, 0] = t if b == 0 else jnp.int32(NT)
        for s in range(DEPTH):
            a = anc[s, 2 * t + b]
            chain[b, 1 + s] = jnp.where(a < 0, -1, jnp.where(a % 2 == 1, NT, a // 2))

    @pl.loop(0, POOL)
    def _(p):
        for b in range(2):
            at = jnp.int32(ZERO_SLOT)
            for s in range(SLOTS):
                at = jnp.where(chain[b, s] == p, s, at)
            inverse[b, p] = at

    parts[:, ZERO_SLOT] = jnp.zeros((2, BLK, HD), jnp.float32)

    for copy in arrivals[1]:
        copy.wait_recv()
    forward(0, AROUND[:6])
    for d, e in AROUND:
        launch(pool_copy(1, d, e))
    launch(share(1, 0, 0))
    forward(0, AROUND[6:])
    for copy in arrivals[2]:
        copy.wait_recv()
    q = [q_in[4 * b : 4 * b + 4].reshape(ROWS, HD) for b in range(2)]
    qt = [tile.T for tile in q]
    for d, e in [(0, 0)] + AROUND:
        await_share(0, d, e)

    score, dprob, dscore = (score0, score1), (dprob0, dprob1), (dscore0, dscore1)

    def tiles(pool, b, first, count):
        found = [pool[jnp.maximum(chain[b, first + j], 0)] for j in range(count)]
        return found[0] if count == 1 else jnp.concatenate(found, axis=0)

    def rows_of(first, count):
        return pl.ds(first * BLK, count * BLK)

    def sweep(step, state):
        state = step(0, 1, state)
        return lax.fori_loop(0, DEPTH // GS, lambda n, state: step(1 + n * GS, GS, state), state)

    def beside(one, two):
        return lambda first, count, state: (one(first, count, state[0]), two(first, count, state[1]))

    def look(b):
        def step(first, count, top):
            s = f32_dot(tiles(kpool, b, first, count), qt[b])
            for j in range(count):
                part = s[j * BLK : (j + 1) * BLK]
                if count == 1:
                    key = lax.broadcasted_iota(jnp.int32, (BLK, ROWS), 0)
                    row = lax.broadcasted_iota(jnp.int32, (BLK, ROWS), 1)
                    part = jnp.where(key * GROUP <= row, part, HIDDEN)
                else:
                    part = part + jnp.where(chain[b, first + j] >= 0, 0.0, HIDDEN)
                score[b][rows_of(first + j, 1), :] = part
                top = jnp.maximum(top, fold(part, jnp.max))
            return top

        return step

    def top_of(top):
        return jnp.max(top, axis=0, keepdims=True) * SCALE2

    def soften(b, top):
        def step(first, count, total):
            e = jnp.exp2(score[b][rows_of(first, count), :] * SCALE2 - top)
            score[b][rows_of(first, count), :] = e
            return total + fold(e, jnp.sum)

        return step

    def over_of(total):
        return 1.0 / jnp.sum(total, axis=0, keepdims=True)

    def value_part(b, over):
        def step(first, count, state):
            p = score[b][rows_of(first, count), :] * over
            dv = f32_dot(p.astype(jnp.bfloat16), g[b])
            for j in range(count):
                parts[b, first + j] = dv[j * BLK : (j + 1) * BLK]
            return state

        return step

    def cross(b):
        def step(first, count, weighted):
            dp = f32_dot(tiles(vpool, b, first, count), gt[b])
            dprob[b][rows_of(first, count), :] = dp
            return weighted + fold(score[b][rows_of(first, count), :] * dp, jnp.sum)

        return step

    def key_part(b, over, delta):
        def step(first, count, state):
            p = score[b][rows_of(first, count), :] * over
            ds = (p * (dprob[b][rows_of(first, count), :] - delta)).astype(jnp.bfloat16)
            dscore[b][rows_of(first, count), :] = ds
            dk = f32_dot(ds, q[b]) * FACTOR
            for j in range(count):
                parts[b, first + j] = dk[j * BLK : (j + 1) * BLK]
            return state

        return step

    def query_part(b):
        def step(first, count, dqt):
            return dqt + lax.dot_general(
                tiles(kpool, b, first, count), dscore[b][rows_of(first, count), :],
                (((0,), (0,)), ((), ())), preferred_element_type=jnp.float32,
            )

        return step

    halves = (dkpool, dvpool)

    def total_of(p):
        return parts[0, inverse[0, p]] + parts[1, inverse[1, p]]

    def half_copy(i, d, e):
        return remote(
            halves[i].at[d * NY + e], core_in.at[i, d, e], half_send.at[i, d, e], half_recv.at[i, d, e], tok=sibling
        )

    def rs_copy(i, d, e):
        return remote(
            plane.at[i, d, e], rs_in.at[i, d, e], rs_send.at[i, d, e], rs_recv.at[i, d, e], tok=tok_at(x + d, y + e, c)
        )

    def give_halves(i):
        for d, e in AROUND + [(0, 0)]:
            halves[i][d * NY + e] = total_of(tok_at(x + d, y + e, 1 - c)).astype(jnp.bfloat16)
            launch(half_copy(i, d, e))

    def give_homes(i):
        for d, e in AROUND:
            mine = total_of(tok_at(x + d, y + e, c))
            half_copy(i, d, e).wait_recv()
            plane[i, d, e] = (mine + core_in[i, d, e].astype(jnp.float32)).astype(jnp.bfloat16)
            launch(rs_copy(i, d, e))
        mine = total_of(t)
        half_copy(i, 0, 0).wait_recv()
        home[i, 4:8] = total_of(NT).astype(jnp.bfloat16).reshape(4, SLICE, HD)
        return mine + core_in[i, 0, 0].astype(jnp.float32)

    def to_tokens(i, total):
        for d, e in AROUND:
            rs_copy(i, d, e).wait_recv()
            total = total + rs_in[i, d, e].astype(jnp.float32)
        home[i, 0:4] = total.astype(jnp.bfloat16).reshape(4, SLICE, HD)
        copies = []
        for dz in Z_ORDER:
            to = (z + dz) % HEADS
            copies.append(launch(remote(home.at[i, to], home_in.at[i, z], home_send.at[i, dz], home_recv.at[i, dz], head=to)))
        home_in[i, z] = home[i, z]
        return copies

    start = jnp.full((8, ROWS), HIDDEN, jnp.float32)
    zero = jnp.zeros((8, ROWS), jnp.float32)
    none = jnp.int32(0)
    top0 = top_of(sweep(look(0), start))
    total0, top1 = sweep(beside(soften(0, top0), look(1)), (zero, start))
    over0, top1 = over_of(total0), top_of(top1)
    total1 = sweep(soften(1, top1), zero)
    over1 = over_of(total1)
    for copy in arrivals[3]:
        copy.wait_recv()
    g = [g_in[4 * b : 4 * b + 4].reshape(ROWS, HD) for b in range(2)]
    gt = [tile.T for tile in g]
    sweep(beside(value_part(0, over0), value_part(1, over1)), (none, none))
    give_halves(1)
    forward(1, AROUND)
    mine_v = give_homes(1)
    for d, e in [(0, 0)] + AROUND:
        await_share(1, d, e)
    weighted0 = sweep(cross(0), zero)
    delta0 = jnp.sum(weighted0, axis=0, keepdims=True) * over0
    _, weighted1 = sweep(beside(key_part(0, over0, delta0), cross(1)), (none, zero))
    delta1 = jnp.sum(weighted1, axis=0, keepdims=True) * over1
    sweep(key_part(1, over1, delta1), none)
    give_halves(0)

    empty = jnp.zeros((HD, ROWS), jnp.float32)
    dqt = sweep(beside(query_part(0), query_part(1)), (empty, empty))
    for b in range(2):
        dqs[4 * b : 4 * b + 4] = (dqt[b] * FACTOR).T.astype(jnp.bfloat16).reshape(4, SLICE * GROUP, HD)
    mine_k = give_homes(0)
    dq_copies = []
    for dz in Z_ORDER:
        to = (z + dz) % HEADS
        dq_copies.append(launch(remote(dqs.at[to], dq_in.at[z], dq_send.at[dz], dq_recv.at[dz], head=to)))
    dq_in[z] = dqs[z]
    v_copies = to_tokens(1, mine_v)
    settle()
    k_copies = to_tokens(0, mine_k)

    picks = one_hot(regroup)
    for copy in dq_copies:
        copy.wait_recv()
    for o in range(4):
        moved = dq_in[:, o * 32 : (o + 1) * 32, :].reshape(256, HD)
        gq_ref[o * 256 : (o + 1) * 256, :] = exact_dot(picks, moved)
    picks = one_hot(kv_tokens_first)
    for copy in v_copies:
        copy.wait_recv()
    gv_ref[...] = exact_dot(picks, home_in[1].reshape(256, HD))
    for copy in k_copies:
        copy.wait_recv()
    gk_ref[...] = exact_dot(picks, home_in[0].reshape(256, HD))
    settle()


def store_kernel(gq, gk, gv, gq_out, gk_out, gv_out, sem):
    copies = [
        pltpu.make_async_copy(src, dst, sem.at[i])
        for i, (src, dst) in enumerate(((gq, gq_out), (gk, gk_out), (gv, gv_out)))
    ]
    for copy in copies:
        copy.start()
    for copy in copies:
        copy.wait()


def whole():
    return pl.BlockSpec(memory_space=pltpu.VMEM)


def anywhere():
    return pl.BlockSpec(memory_space=pl.ANY)


def shape(*dims):
    return jax.ShapeDtypeStruct(dims, jnp.bfloat16)


def buffer(*dims, dtype=jnp.bfloat16):
    return pltpu.VMEM(dims, dtype)


def sems(*dims):
    return pltpu.SemaphoreType.DMA(dims)


def local(queries, keys, values, grad_out, ancestry):
    rows = SLICE * GROUP
    results = (shape(SLICE * 32, HD), shape(SLICE * HEADS, HD), shape(SLICE * HEADS, HD))
    grads = pl.pallas_call(
        kernel,
        out_shape=tuple(pltpu.VMEM(r.shape, r.dtype) for r in results),
        in_specs=[anywhere()] * 5,
        out_specs=(whole(),) * 3,
        scratch_shapes=[
            pltpu.SMEM((DEPTH, 2 * NT), jnp.int32),
            buffer(SLICE * 32, HD), buffer(SLICE * HEADS, HD), buffer(SLICE * HEADS, HD), buffer(SLICE * 32, HD),
            sems(5),
            buffer(HEADS, SLICE, HD), buffer(HEADS, SLICE, HD), buffer(HEADS, rows, HD), buffer(HEADS, rows, HD),
            buffer(HEADS, rows, HD), buffer(HEADS, rows, HD), buffer(POOL, BLK, HD), buffer(POOL, BLK, HD),
            pltpu.SMEM((2, SLOTS), jnp.int32), pltpu.SMEM((2, POOL), jnp.int32),
            buffer(KEYS, ROWS, dtype=jnp.float32), buffer(KEYS, ROWS, dtype=jnp.float32),
            buffer(KEYS, ROWS, dtype=jnp.float32), buffer(KEYS, ROWS, dtype=jnp.float32),
            buffer(KEYS, ROWS), buffer(KEYS, ROWS),
            buffer(2, SLOTS + 1, BLK, HD, dtype=jnp.float32),
            buffer(NX * NY, BLK, HD), buffer(NX * NY, BLK, HD),
            buffer(2, NX, NY, BLK, HD), buffer(2, NX, NY, BLK, HD), buffer(2, NX, NY, BLK, HD),
            buffer(2, HEADS, SLICE, HD), buffer(2, HEADS, SLICE, HD), buffer(HEADS, rows, HD), buffer(HEADS, rows, HD),
            sems(4, 8), sems(4, 8), sems(2, 4, 4), sems(2, 4, 4), sems(2, 4, 4), sems(2, 4, 4),
            sems(2, 4, 4), sems(2, 4, 4), sems(2, 4, 4), sems(2, 4, 4), sems(2, 8), sems(2, 8), sems(8), sems(8),
        ],
        compiler_params=pltpu.CompilerParams(collective_id=0, has_side_effects=True, vmem_limit_bytes=VMEM_LIMIT),
        name="backward",
    )(
        ancestry.T,
        queries.reshape(SLICE * 32, HD),
        keys.reshape(SLICE * HEADS, HD),
        values.reshape(SLICE * HEADS, HD),
        grad_out.reshape(SLICE * 32, HD),
    )
    gq, gk, gv = pl.pallas_call(
        store_kernel,
        out_shape=results,
        in_specs=[whole()] * 3,
        out_specs=(anywhere(),) * 3,
        scratch_shapes=[sems(3)],
        name="store",
    )(*(pltpu.with_memory_space_constraint(r, pltpu.VMEM) for r in grads))
    return (
        gq.reshape(SLICE, 32, HD),
        gk.reshape(SLICE, HEADS, HD),
        gv.reshape(SLICE, HEADS, HD),
    )


def solution(mesh):
    placed = P(("tok", "head"), None, None)
    return jax.shard_map(
        local,
        mesh=mesh,
        in_specs=(placed, placed, placed, placed, P()),
        out_specs=(placed, placed, placed),
        check_vma=False,
    )
```

```python
import math

import jax
import jax.numpy as jnp
from jax import lax
from jax.experimental import pallas as pl
from jax.experimental.pallas import tpu as pltpu
from jax.sharding import PartitionSpec as P

BLK = 128
HD = 128
GROUP = 4
HEADS = 8
NX, NY, NC = 4, 4, 2
NT = NX * NY * NC
SLICE = 32
DEPTH = 16
SLOTS = DEPTH + 1
ZERO_SLOT = SLOTS
POOL = NT + 1
ROWS = BLK * GROUP
KEYS = SLOTS * BLK
FACTOR = 1.0 / math.sqrt(HD)
SCALE2 = FACTOR * math.log2(math.e)
HIDDEN = -1e30
GS = 8
Z_ORDER = (4, 3, 5, 2, 6, 1, 7)
AROUND = sorted(((d, e) for d in range(NX) for e in range(NY) if d or e), key=lambda o: -sum(min(n, 4 - n) for n in o))
VMEM_LIMIT = 56 * 1024 * 1024
MESH = pl.DeviceIdType.MESH


def remote(src, dst, send_sem, recv_sem, **where):
    return pltpu.make_async_remote_copy(
        src_ref=src,
        dst_ref=dst,
        send_sem=send_sem,
        recv_sem=recv_sem,
        device_id=where,
        device_id_type=MESH,
    )


def tok_at(x, y, c):
    return (x % NX) * (NY * NC) + (y % NY) * NC + c


def one_hot(source):
    rows = lax.broadcasted_iota(jnp.int32, (256, 256), 0)
    cols = lax.broadcasted_iota(jnp.int32, (256, 256), 1)
    return jnp.where(source(rows) == cols, 1.0, 0.0).astype(jnp.bfloat16)


def exact_dot(picks, rows):
    return jnp.dot(picks, rows, preferred_element_type=jnp.float32).astype(jnp.bfloat16)


def regroup(i):
    return (i // 4 % 8) * 32 + (i // 32) * 4 + i % 4


def kv_heads_first(i):
    return (i % 32) * 8 + i // 32


def kv_tokens_first(i):
    return (i % 8) * 32 + i // 8


def fold(tile, op):
    return op(tile.reshape(-1, 8, ROWS), axis=0)


def f32_dot(a, b):
    return jnp.dot(a, b, preferred_element_type=jnp.float32)


def kernel(
    anc_hbm, q_hbm, k_hbm, v_hbm, g_hbm,
    gq_ref, gk_ref, gv_ref,
    anc, q_raw, k_raw, v_raw, g_raw, load_sem,
    ks, vs, qs, gs, q_in, g_in, kpool, vpool,
    chain, inverse, score0, score1, dprob0, dprob1, dscore0, dscore1, parts,
    dvpool, dkpool, core_in, plane, rs_in, home, home_in, dqs, dq_in,
    in_send, in_recv, pool_send, pool_recv, share_send, share_recv,
    half_send, half_recv, rs_send, rs_recv, home_send, home_recv, dq_send, dq_recv,
):
    t = lax.axis_index("tok")
    z = lax.axis_index("head")
    x, y, c = t // (NY * NC), (t // NC) % NY, t % NC
    sibling = tok_at(x, y, 1 - c)
    sent = []

    def launch(copy):
        copy.start()
        sent.append(copy)
        return copy

    def settle():
        while sent:
            sent.pop(0).wait_send()

    loads = []
    for i, (src, dst) in enumerate(((k_hbm, k_raw), (v_hbm, v_raw), (q_hbm, q_raw), (g_hbm, g_raw), (anc_hbm, anc))):
        load = pltpu.make_async_copy(src, dst, load_sem.at[i])
        load.start()
        loads.append(load)
    barrier = pltpu.get_barrier_semaphore()
    for dz in range(1, HEADS):
        pl.semaphore_signal(barrier, inc=1, device_id={"head": (z + dz) % HEADS}, device_id_type=MESH)
    for d, e in AROUND:
        pl.semaphore_signal(barrier, inc=1, device_id={"tok": tok_at(x + d, y + e, c)}, device_id_type=MESH)
    pl.semaphore_signal(barrier, inc=1, device_id={"tok": sibling}, device_id_type=MESH)

    slot = jnp.where(z < 4, t, NT)
    rows = pl.ds(pl.multiple_of((z % 4) * SLICE, SLICE), SLICE)
    arrivals = [[], [], [], []]

    def send_kv(i, src, pool):
        for dz in Z_ORDER:
            to = (z + dz) % HEADS
            copy = remote(src.at[to], pool.at[slot, rows, :], in_send.at[i, dz], in_recv.at[i, dz], head=to)
            arrivals[i].append(launch(copy))

    def send_heads(i, src, into):
        for dz in Z_ORDER:
            to = (z + dz) % HEADS
            copy = remote(src.at[to], into.at[z], in_send.at[i, dz], in_recv.at[i, dz], head=to)
            arrivals[i].append(launch(copy))

    def group_kv(i, raw, out, pool):
        loads[i].wait()
        out[...] = exact_dot(kv_picks, raw[...]).reshape(HEADS, SLICE, HD)
        pool[slot, rows, :] = out[z]

    def group_heads(i, raw, out, into):
        loads[i].wait()
        for o in range(4):
            moved = exact_dot(picks, raw[o * 256 : (o + 1) * 256, :])
            out[:, o * 32 : (o + 1) * 32, :] = moved.reshape(HEADS, 32, HD)
        into[z] = out[z]

    kv_picks = one_hot(kv_heads_first)
    group_kv(0, k_raw, ks, kpool)
    pl.semaphore_wait(barrier, HEADS - 1 + len(AROUND) + 1)
    send_kv(0, ks, kpool)
    picks = one_hot(regroup)
    group_heads(2, q_raw, qs, q_in)
    send_heads(2, qs, q_in)
    group_kv(1, v_raw, vs, vpool)
    send_kv(1, vs, vpool)
    group_heads(3, g_raw, gs, g_in)
    send_heads(3, gs, g_in)

    pools = (kpool, vpool)

    def pool_copy(i, d, e):
        ref = pools[i].at[t]
        return remote(ref, ref, pool_send.at[i, d, e], pool_recv.at[i, d, e], tok=tok_at(x + d, y + e, c))

    def share(i, d, e):
        ref = pools[i].at[tok_at(x - d, y - e, c)]
        return remote(ref, ref, share_send.at[i, d, e], share_recv.at[i, d, e], tok=sibling)

    def await_pool(i, d, e):
        ref = pools[i].at[tok_at(x - d, y - e, c)]
        remote(ref, ref, pool_send.at[i, d, e], pool_recv.at[i, d, e], tok=t).wait_recv()

    def await_share(i, d, e):
        ref = pools[i].at[tok_at(x - d, y - e, 1 - c)]
        remote(ref, ref, share_send.at[i, d, e], share_recv.at[i, d, e], tok=t).wait_recv()

    def forward(i, offsets):
        for d, e in offsets:
            await_pool(i, d, e)
            launch(share(i, d, e))

    for copy in arrivals[0]:
        copy.wait_recv()
    for d, e in AROUND:
        launch(pool_copy(0, d, e))
    launch(share(0, 0, 0))
    loads[4].wait()
    for b in range(2):
        chain[b, 0] = t if b == 0 else jnp.int32(NT)
        for s in range(DEPTH):
            a = anc[s, 2 * t + b]
            chain[b, 1 + s] = jnp.where(a < 0, -1, jnp.where(a % 2 == 1, NT, a // 2))

    @pl.loop(0, POOL)
    def _(p):
        for b in range(2):
            at = jnp.int32(ZERO_SLOT)
            for s in range(SLOTS):
                at = jnp.where(chain[b, s] == p, s, at)
            inverse[b, p] = at

    parts[:, ZERO_SLOT] = jnp.zeros((2, BLK, HD), jnp.float32)

    for copy in arrivals[1]:
        copy.wait_recv()
    forward(0, AROUND[:15])
    for d, e in AROUND:
        launch(pool_copy(1, d, e))
    launch(share(1, 0, 0))
    forward(0, AROUND[15:])
    for copy in arrivals[2]:
        copy.wait_recv()
    q = [q_in[4 * b : 4 * b + 4].reshape(ROWS, HD) for b in range(2)]
    qt = [tile.T for tile in q]
    for d, e in [(0, 0)] + AROUND:
        await_share(0, d, e)

    score, dprob, dscore = (score0, score1), (dprob0, dprob1), (dscore0, dscore1)

    def tiles(pool, b, first, count):
        found = [pool[jnp.maximum(chain[b, first + j], 0)] for j in range(count)]
        return found[0] if count == 1 else jnp.concatenate(found, axis=0)

    def rows_of(first, count):
        return pl.ds(first * BLK, count * BLK)

    def sweep(step, state):
        state = step(0, 1, state)
        return lax.fori_loop(0, DEPTH // GS, lambda n, state: step(1 + n * GS, GS, state), state)

    def beside(one, two):
        return lambda first, count, state: (one(first, count, state[0]), two(first, count, state[1]))

    def look(b):
        def step(first, count, top):
            s = f32_dot(tiles(kpool, b, first, count), qt[b])
            for j in range(count):
                part = s[j * BLK : (j + 1) * BLK]
                if count == 1:
                    key = lax.broadcasted_iota(jnp.int32, (BLK, ROWS), 0)
                    row = lax.broadcasted_iota(jnp.int32, (BLK, ROWS), 1)
                    part = jnp.where(key * GROUP <= row, part, HIDDEN)
                else:
                    part = part + jnp.where(chain[b, first + j] >= 0, 0.0, HIDDEN)
                score[b][rows_of(first + j, 1), :] = part
                top = jnp.maximum(top, fold(part, jnp.max))
            return top

        return step

    def top_of(top):
        return jnp.max(top, axis=0, keepdims=True) * SCALE2

    def soften(b, top):
        def step(first, count, total):
            e = jnp.exp2(score[b][rows_of(first, count), :] * SCALE2 - top)
            score[b][rows_of(first, count), :] = e
            return total + fold(e, jnp.sum)

        return step

    def over_of(total):
        return 1.0 / jnp.sum(total, axis=0, keepdims=True)

    def value_part(b, over):
        def step(first, count, state):
            p = score[b][rows_of(first, count), :] * over
            dv = f32_dot(p.astype(jnp.bfloat16), g[b])
            for j in range(count):
                parts[b, first + j] = dv[j * BLK : (j + 1) * BLK]
            return state

        return step

    def cross(b):
        def step(first, count, weighted):
            dp = f32_dot(tiles(vpool, b, first, count), gt[b])
            dprob[b][rows_of(first, count), :] = dp
            return weighted + fold(score[b][rows_of(first, count), :] * dp, jnp.sum)

        return step

    def key_part(b, over, delta):
        def step(first, count, state):
            p = score[b][rows_of(first, count), :] * over
            ds = (p * (dprob[b][rows_of(first, count), :] - delta)).astype(jnp.bfloat16)
            dscore[b][rows_of(first, count), :] = ds
            dk = f32_dot(ds, q[b]) * FACTOR
            for j in range(count):
                parts[b, first + j] = dk[j * BLK : (j + 1) * BLK]
            return state

        return step

    def query_part(b):
        def step(first, count, dqt):
            return dqt + lax.dot_general(
                tiles(kpool, b, first, count), dscore[b][rows_of(first, count), :],
                (((0,), (0,)), ((), ())), preferred_element_type=jnp.float32,
            )

        return step

    halves = (dkpool, dvpool)

    def total_of(p):
        return parts[0, inverse[0, p]] + parts[1, inverse[1, p]]

    def half_copy(i, d, e):
        return remote(
            halves[i].at[d * NY + e], core_in.at[i, d, e], half_send.at[i, d, e], half_recv.at[i, d, e], tok=sibling
        )

    def rs_copy(i, d, e):
        return remote(
            plane.at[i, d, e], rs_in.at[i, d, e], rs_send.at[i, d, e], rs_recv.at[i, d, e], tok=tok_at(x + d, y + e, c)
        )

    def give_halves(i):
        for d, e in AROUND + [(0, 0)]:
            halves[i][d * NY + e] = total_of(tok_at(x + d, y + e, 1 - c)).astype(jnp.bfloat16)
            launch(half_copy(i, d, e))

    def give_homes(i):
        for d, e in AROUND:
            mine = total_of(tok_at(x + d, y + e, c))
            half_copy(i, d, e).wait_recv()
            plane[i, d, e] = (mine + core_in[i, d, e].astype(jnp.float32)).astype(jnp.bfloat16)
            launch(rs_copy(i, d, e))
        mine = total_of(t)
        half_copy(i, 0, 0).wait_recv()
        home[i, 4:8] = total_of(NT).astype(jnp.bfloat16).reshape(4, SLICE, HD)
        return mine + core_in[i, 0, 0].astype(jnp.float32)

    def to_tokens(i, total):
        for d, e in AROUND:
            rs_copy(i, d, e).wait_recv()
            total = total + rs_in[i, d, e].astype(jnp.float32)
        home[i, 0:4] = total.astype(jnp.bfloat16).reshape(4, SLICE, HD)
        copies = []
        for dz in Z_ORDER:
            to = (z + dz) % HEADS
            copies.append(launch(remote(home.at[i, to], home_in.at[i, z], home_send.at[i, dz], home_recv.at[i, dz], head=to)))
        home_in[i, z] = home[i, z]
        return copies

    start = jnp.full((8, ROWS), HIDDEN, jnp.float32)
    zero = jnp.zeros((8, ROWS), jnp.float32)
    none = jnp.int32(0)
    top0, top1 = sweep(beside(look(0), look(1)), (start, start))
    total0, total1 = sweep(beside(soften(0, top_of(top0)), soften(1, top_of(top1))), (zero, zero))
    over0, over1 = over_of(total0), over_of(total1)
    for copy in arrivals[3]:
        copy.wait_recv()
    g = [g_in[4 * b : 4 * b + 4].reshape(ROWS, HD) for b in range(2)]
    sweep(beside(value_part(0, over0), value_part(1, over1)), (none, none))
    give_halves(1)
    gt = [tile.T for tile in g]
    forward(1, AROUND)
    mine_v = give_homes(1)
    for d, e in [(0, 0)] + AROUND:
        await_share(1, d, e)
    weighted = sweep(beside(cross(0), cross(1)), (zero, zero))
    delta0 = jnp.sum(weighted[0], axis=0, keepdims=True) * over0
    delta1 = jnp.sum(weighted[1], axis=0, keepdims=True) * over1
    sweep(beside(key_part(0, over0, delta0), key_part(1, over1, delta1)), (none, none))
    give_halves(0)

    empty = jnp.zeros((HD, ROWS), jnp.float32)
    dqt = sweep(beside(query_part(0), query_part(1)), (empty, empty))
    for b in range(2):
        dqs[4 * b : 4 * b + 4] = (dqt[b] * FACTOR).T.astype(jnp.bfloat16).reshape(4, SLICE * GROUP, HD)
    mine_k = give_homes(0)
    dq_copies = []
    for dz in Z_ORDER:
        to = (z + dz) % HEADS
        dq_copies.append(launch(remote(dqs.at[to], dq_in.at[z], dq_send.at[dz], dq_recv.at[dz], head=to)))
    dq_in[z] = dqs[z]
    v_copies = to_tokens(1, mine_v)
    settle()
    k_copies = to_tokens(0, mine_k)

    picks = one_hot(regroup)
    for copy in dq_copies:
        copy.wait_recv()
    for o in range(4):
        moved = dq_in[:, o * 32 : (o + 1) * 32, :].reshape(256, HD)
        gq_ref[o * 256 : (o + 1) * 256, :] = exact_dot(picks, moved)
    picks = one_hot(kv_tokens_first)
    for copy in v_copies:
        copy.wait_recv()
    gv_ref[...] = exact_dot(picks, home_in[1].reshape(256, HD))
    for copy in k_copies:
        copy.wait_recv()
    gk_ref[...] = exact_dot(picks, home_in[0].reshape(256, HD))
    settle()


def store_kernel(gq, gk, gv, gq_out, gk_out, gv_out, sem):
    copies = [
        pltpu.make_async_copy(src, dst, sem.at[i])
        for i, (src, dst) in enumerate(((gq, gq_out), (gk, gk_out), (gv, gv_out)))
    ]
    for copy in copies:
        copy.start()
    for copy in copies:
        copy.wait()


def whole():
    return pl.BlockSpec(memory_space=pltpu.VMEM)


def anywhere():
    return pl.BlockSpec(memory_space=pl.ANY)


def shape(*dims):
    return jax.ShapeDtypeStruct(dims, jnp.bfloat16)


def buffer(*dims, dtype=jnp.bfloat16):
    return pltpu.VMEM(dims, dtype)


def sems(*dims):
    return pltpu.SemaphoreType.DMA(dims)


def local(queries, keys, values, grad_out, ancestry):
    rows = SLICE * GROUP
    results = (shape(SLICE * 32, HD), shape(SLICE * HEADS, HD), shape(SLICE * HEADS, HD))
    grads = pl.pallas_call(
        kernel,
        out_shape=tuple(pltpu.VMEM(r.shape, r.dtype) for r in results),
        in_specs=[anywhere()] * 5,
        out_specs=(whole(),) * 3,
        scratch_shapes=[
            pltpu.SMEM((DEPTH, 2 * NT), jnp.int32),
            buffer(SLICE * 32, HD), buffer(SLICE * HEADS, HD), buffer(SLICE * HEADS, HD), buffer(SLICE * 32, HD),
            sems(5),
            buffer(HEADS, SLICE, HD), buffer(HEADS, SLICE, HD), buffer(HEADS, rows, HD), buffer(HEADS, rows, HD),
            buffer(HEADS, rows, HD), buffer(HEADS, rows, HD), buffer(POOL, BLK, HD), buffer(POOL, BLK, HD),
            pltpu.SMEM((2, SLOTS), jnp.int32), pltpu.SMEM((2, POOL), jnp.int32),
            buffer(KEYS, ROWS, dtype=jnp.float32), buffer(KEYS, ROWS, dtype=jnp.float32),
            buffer(KEYS, ROWS, dtype=jnp.float32), buffer(KEYS, ROWS, dtype=jnp.float32),
            buffer(KEYS, ROWS), buffer(KEYS, ROWS),
            buffer(2, SLOTS + 1, BLK, HD, dtype=jnp.float32),
            buffer(NX * NY, BLK, HD), buffer(NX * NY, BLK, HD),
            buffer(2, NX, NY, BLK, HD), buffer(2, NX, NY, BLK, HD), buffer(2, NX, NY, BLK, HD),
            buffer(2, HEADS, SLICE, HD), buffer(2, HEADS, SLICE, HD), buffer(HEADS, rows, HD), buffer(HEADS, rows, HD),
            sems(4, 8), sems(4, 8), sems(2, 4, 4), sems(2, 4, 4), sems(2, 4, 4), sems(2, 4, 4),
            sems(2, 4, 4), sems(2, 4, 4), sems(2, 4, 4), sems(2, 4, 4), sems(2, 8), sems(2, 8), sems(8), sems(8),
        ],
        compiler_params=pltpu.CompilerParams(collective_id=0, has_side_effects=True, vmem_limit_bytes=VMEM_LIMIT),
        name="backward",
    )(
        ancestry.T,
        queries.reshape(SLICE * 32, HD),
        keys.reshape(SLICE * HEADS, HD),
        values.reshape(SLICE * HEADS, HD),
        grad_out.reshape(SLICE * 32, HD),
    )
    gq, gk, gv = pl.pallas_call(
        store_kernel,
        out_shape=results,
        in_specs=[whole()] * 3,
        out_specs=(anywhere(),) * 3,
        scratch_shapes=[sems(3)],
        name="store",
    )(*(pltpu.with_memory_space_constraint(r, pltpu.VMEM) for r in grads))
    return (
        gq.reshape(SLICE, 32, HD),
        gk.reshape(SLICE, HEADS, HD),
        gv.reshape(SLICE, HEADS, HD),
    )


def solution(mesh):
    placed = P(("tok", "head"), None, None)
    return jax.shard_map(
        local,
        mesh=mesh,
        in_specs=(placed, placed, placed, placed, P()),
        out_specs=(placed, placed, placed),
        check_vma=False,
    )
```

```python
import math

import jax
import jax.numpy as jnp
from jax import lax
from jax.experimental import pallas as pl
from jax.experimental.pallas import tpu as pltpu
from jax.sharding import PartitionSpec as P

BLK = 128
HD = 128
GROUP = 4
HEADS = 8
NX, NY, NC = 4, 4, 2
NT = NX * NY * NC
SLICE = 32
DEPTH = 16
SLOTS = DEPTH + 1
ZERO_SLOT = SLOTS
POOL = NT + 1
ROWS = BLK * GROUP
KEYS = SLOTS * BLK
FACTOR = 1.0 / math.sqrt(HD)
SCALE2 = FACTOR * math.log2(math.e)
HIDDEN = -1e30
GS = 8
Z_ORDER = (4, 3, 5, 2, 6, 1, 7)
AROUND = sorted(((d, e) for d in range(NX) for e in range(NY) if d or e), key=lambda o: -sum(min(n, 4 - n) for n in o))
NEAR = AROUND[::-1]
VMEM_LIMIT = 56 * 1024 * 1024
MESH = pl.DeviceIdType.MESH


def remote(src, dst, send_sem, recv_sem, **where):
    return pltpu.make_async_remote_copy(
        src_ref=src,
        dst_ref=dst,
        send_sem=send_sem,
        recv_sem=recv_sem,
        device_id=where,
        device_id_type=MESH,
    )


def tok_at(x, y, c):
    return (x % NX) * (NY * NC) + (y % NY) * NC + c


def one_hot(source):
    rows = lax.broadcasted_iota(jnp.int32, (256, 256), 0)
    cols = lax.broadcasted_iota(jnp.int32, (256, 256), 1)
    return jnp.where(source(rows) == cols, 1.0, 0.0).astype(jnp.bfloat16)


def exact_dot(picks, rows):
    return jnp.dot(picks, rows, preferred_element_type=jnp.float32).astype(jnp.bfloat16)


def regroup(i):
    return (i // 4 % 8) * 32 + (i // 32) * 4 + i % 4


def kv_heads_first(i):
    return (i % 32) * 8 + i // 32


def kv_tokens_first(i):
    return (i % 8) * 32 + i // 8


def fold(tile, op):
    return op(tile.reshape(-1, 8, ROWS), axis=0)


def f32_dot(a, b):
    return jnp.dot(a, b, preferred_element_type=jnp.float32)


def kernel(
    anc_hbm, q_hbm, k_hbm, v_hbm, g_hbm,
    gq_ref, gk_ref, gv_ref,
    anc, q_raw, k_raw, v_raw, g_raw, load_sem,
    ks, vs, qs, gs, q_in, g_in, kpool, vpool,
    chain, inverse, score0, score1, dprob0, dprob1, dscore0, dscore1, parts,
    dvpool, dkpool, core_in, plane, rs_in, home, home_in, dqs, dq_in,
    in_send, in_recv, pool_send, pool_recv, share_send, share_recv,
    half_send, half_recv, rs_send, rs_recv, home_send, home_recv, dq_send, dq_recv,
):
    t = lax.axis_index("tok")
    z = lax.axis_index("head")
    x, y, c = t // (NY * NC), (t // NC) % NY, t % NC
    sibling = tok_at(x, y, 1 - c)
    sent = []

    def launch(copy):
        copy.start()
        sent.append(copy)
        return copy

    def settle():
        while sent:
            sent.pop(0).wait_send()

    barrier = pltpu.get_barrier_semaphore()
    for dz in Z_ORDER:
        pl.semaphore_signal(barrier, inc=1, device_id={"head": (z + dz) % HEADS}, device_id_type=MESH)
    for d, e in AROUND:
        pl.semaphore_signal(barrier, inc=1, device_id={"tok": tok_at(x + d, y + e, c)}, device_id_type=MESH)
    pl.semaphore_signal(barrier, inc=1, device_id={"tok": sibling}, device_id_type=MESH)
    loads = []
    for i, (src, dst) in enumerate(((k_hbm, k_raw), (v_hbm, v_raw), (q_hbm, q_raw), (g_hbm, g_raw), (anc_hbm, anc))):
        load = pltpu.make_async_copy(src, dst, load_sem.at[i])
        load.start()
        loads.append(load)

    slot = jnp.where(z < 4, t, NT)
    rows = pl.ds(pl.multiple_of((z % 4) * SLICE, SLICE), SLICE)
    arrivals = [[], [], [], []]

    def send_kv(i, src, pool):
        for dz in Z_ORDER:
            to = (z + dz) % HEADS
            copy = remote(src.at[to], pool.at[slot, rows, :], in_send.at[i, dz], in_recv.at[i, dz], head=to)
            arrivals[i].append(launch(copy))

    def send_heads(i, src, into):
        for dz in Z_ORDER:
            to = (z + dz) % HEADS
            copy = remote(src.at[to], into.at[z], in_send.at[i, dz], in_recv.at[i, dz], head=to)
            arrivals[i].append(launch(copy))

    def group_kv(i, raw, out, pool):
        loads[i].wait()
        out[...] = exact_dot(kv_picks, raw[...]).reshape(HEADS, SLICE, HD)
        pool[slot, rows, :] = out[z]

    def group_heads(i, raw, out, into):
        loads[i].wait()
        for o in range(4):
            moved = exact_dot(picks, raw[o * 256 : (o + 1) * 256, :])
            out[:, o * 32 : (o + 1) * 32, :] = moved.reshape(HEADS, 32, HD)
        into[z] = out[z]

    kv_picks = one_hot(kv_heads_first)
    group_kv(0, k_raw, ks, kpool)
    pl.semaphore_wait(barrier, HEADS - 1 + len(AROUND) + 1)
    send_kv(0, ks, kpool)
    picks = one_hot(regroup)
    group_heads(2, q_raw, qs, q_in)
    send_heads(2, qs, q_in)
    group_kv(1, v_raw, vs, vpool)
    send_kv(1, vs, vpool)
    group_heads(3, g_raw, gs, g_in)
    send_heads(3, gs, g_in)

    pools = (kpool, vpool)

    def pool_copy(i, d, e):
        ref = pools[i].at[t]
        return remote(ref, ref, pool_send.at[i, d, e], pool_recv.at[i, d, e], tok=tok_at(x + d, y + e, c))

    def share(i, d, e):
        ref = pools[i].at[tok_at(x - d, y - e, c)]
        return remote(ref, ref, share_send.at[i, d, e], share_recv.at[i, d, e], tok=sibling)

    def await_pool(i, d, e):
        ref = pools[i].at[tok_at(x - d, y - e, c)]
        remote(ref, ref, pool_send.at[i, d, e], pool_recv.at[i, d, e], tok=t).wait_recv()

    def await_share(i, d, e):
        ref = pools[i].at[tok_at(x - d, y - e, 1 - c)]
        remote(ref, ref, share_send.at[i, d, e], share_recv.at[i, d, e], tok=t).wait_recv()

    def forward(i, offsets):
        for d, e in offsets:
            await_pool(i, d, e)
            launch(share(i, d, e))

    for copy in arrivals[0]:
        copy.wait_recv()
    for d, e in AROUND:
        launch(pool_copy(0, d, e))
    launch(share(0, 0, 0))
    loads[4].wait()
    for b in range(2):
        chain[b, 0] = t if b == 0 else jnp.int32(NT)
        for s in range(DEPTH):
            a = anc[s, 2 * t + b]
            chain[b, 1 + s] = jnp.where(a < 0, -1, jnp.where(a % 2 == 1, NT, a // 2))

    @pl.loop(0, POOL)
    def _(p):
        for b in range(2):
            at = jnp.int32(ZERO_SLOT)
            for s in range(SLOTS):
                at = jnp.where(chain[b, s] == p, s, at)
            inverse[b, p] = at

    parts[:, ZERO_SLOT] = jnp.zeros((2, BLK, HD), jnp.float32)

    for copy in arrivals[1]:
        copy.wait_recv()
    for d, e in AROUND:
        launch(pool_copy(1, d, e))
    launch(share(1, 0, 0))
    forward(0, NEAR)
    for copy in arrivals[2]:
        copy.wait_recv()
    q = [q_in[4 * b : 4 * b + 4].reshape(ROWS, HD) for b in range(2)]
    qt = [tile.T for tile in q]
    for d, e in [(0, 0)] + AROUND:
        await_share(0, d, e)

    score, dprob, dscore = (score0, score1), (dprob0, dprob1), (dscore0, dscore1)

    def tiles(pool, b, first, count):
        found = [pool[jnp.maximum(chain[b, first + j], 0)] for j in range(count)]
        return found[0] if count == 1 else jnp.concatenate(found, axis=0)

    def rows_of(first, count):
        return pl.ds(first * BLK, count * BLK)

    def sweep(step, state):
        state = step(0, 1, state)
        return lax.fori_loop(0, DEPTH // GS, lambda n, state: step(1 + n * GS, GS, state), state)

    def beside(one, two):
        return lambda first, count, state: (one(first, count, state[0]), two(first, count, state[1]))

    def look(b):
        def step(first, count, top):
            s = f32_dot(tiles(kpool, b, first, count), qt[b])
            for j in range(count):
                part = s[j * BLK : (j + 1) * BLK]
                if count == 1:
                    key = lax.broadcasted_iota(jnp.int32, (BLK, ROWS), 0)
                    row = lax.broadcasted_iota(jnp.int32, (BLK, ROWS), 1)
                    part = jnp.where(key * GROUP <= row, part, HIDDEN)
                else:
                    part = part + jnp.where(chain[b, first + j] >= 0, 0.0, HIDDEN)
                score[b][rows_of(first + j, 1), :] = part
                top = jnp.maximum(top, fold(part, jnp.max))
            return top

        return step

    def top_of(top):
        return jnp.max(top, axis=0, keepdims=True) * SCALE2

    def soften(b, top):
        def step(first, count, total):
            e = jnp.exp2(score[b][rows_of(first, count), :] * SCALE2 - top)
            score[b][rows_of(first, count), :] = e
            return total + fold(e, jnp.sum)

        return step

    def over_of(total):
        return 1.0 / jnp.sum(total, axis=0, keepdims=True)

    def value_part(b, over):
        def step(first, count, state):
            p = score[b][rows_of(first, count), :] * over
            dv = f32_dot(p.astype(jnp.bfloat16), g[b])
            for j in range(count):
                parts[b, first + j] = dv[j * BLK : (j + 1) * BLK]
            return state

        return step

    def cross(b):
        def step(first, count, weighted):
            dp = f32_dot(tiles(vpool, b, first, count), gt[b])
            dprob[b][rows_of(first, count), :] = dp
            return weighted + fold(score[b][rows_of(first, count), :] * dp, jnp.sum)

        return step

    def key_part(b, over, delta):
        def step(first, count, state):
            p = score[b][rows_of(first, count), :] * over
            ds = (p * (dprob[b][rows_of(first, count), :] - delta)).astype(jnp.bfloat16)
            dscore[b][rows_of(first, count), :] = ds
            dk = f32_dot(ds, q[b]) * FACTOR
            for j in range(count):
                parts[b, first + j] = dk[j * BLK : (j + 1) * BLK]
            return state

        return step

    def query_part(b):
        def step(first, count, dqt):
            return dqt + lax.dot_general(
                tiles(kpool, b, first, count), dscore[b][rows_of(first, count), :],
                (((0,), (0,)), ((), ())), preferred_element_type=jnp.float32,
            )

        return step

    halves = (dkpool, dvpool)

    def total_of(p):
        return parts[0, inverse[0, p]] + parts[1, inverse[1, p]]

    def half_copy(i, d, e):
        return remote(
            halves[i].at[d * NY + e], core_in.at[i, d, e], half_send.at[i, d, e], half_recv.at[i, d, e], tok=sibling
        )

    def rs_copy(i, d, e):
        return remote(
            plane.at[i, d, e], rs_in.at[i, d, e], rs_send.at[i, d, e], rs_recv.at[i, d, e], tok=tok_at(x + d, y + e, c)
        )

    def give_halves(i):
        for d, e in AROUND + [(0, 0)]:
            halves[i][d * NY + e] = total_of(tok_at(x + d, y + e, 1 - c)).astype(jnp.bfloat16)
            launch(half_copy(i, d, e))

    def give_homes(i):
        for d, e in AROUND:
            mine = total_of(tok_at(x + d, y + e, c))
            half_copy(i, d, e).wait_recv()
            plane[i, d, e] = (mine + core_in[i, d, e].astype(jnp.float32)).astype(jnp.bfloat16)
            launch(rs_copy(i, d, e))
        mine = total_of(t)
        half_copy(i, 0, 0).wait_recv()
        home[i, 4:8] = total_of(NT).astype(jnp.bfloat16).reshape(4, SLICE, HD)
        return mine + core_in[i, 0, 0].astype(jnp.float32)

    def to_tokens(i, total):
        for d, e in NEAR:
            rs_copy(i, d, e).wait_recv()
            total = total + rs_in[i, d, e].astype(jnp.float32)
        home[i, 0:4] = total.astype(jnp.bfloat16).reshape(4, SLICE, HD)
        copies = []
        for dz in Z_ORDER:
            to = (z + dz) % HEADS
            copies.append(launch(remote(home.at[i, to], home_in.at[i, z], home_send.at[i, dz], home_recv.at[i, dz], head=to)))
        home_in[i, z] = home[i, z]
        return copies

    start = jnp.full((8, ROWS), HIDDEN, jnp.float32)
    zero = jnp.zeros((8, ROWS), jnp.float32)
    none = jnp.int32(0)
    top0, top1 = sweep(beside(look(0), look(1)), (start, start))
    total0, total1 = sweep(beside(soften(0, top_of(top0)), soften(1, top_of(top1))), (zero, zero))
    over0, over1 = over_of(total0), over_of(total1)
    for copy in arrivals[3]:
        copy.wait_recv()
    g = [g_in[4 * b : 4 * b + 4].reshape(ROWS, HD) for b in range(2)]
    sweep(beside(value_part(0, over0), value_part(1, over1)), (none, none))
    give_halves(1)
    gt = [tile.T for tile in g]
    forward(1, NEAR)
    mine_v = give_homes(1)
    for d, e in [(0, 0)] + AROUND:
        await_share(1, d, e)
    weighted = sweep(beside(cross(0), cross(1)), (zero, zero))
    delta0 = jnp.sum(weighted[0], axis=0, keepdims=True) * over0
    delta1 = jnp.sum(weighted[1], axis=0, keepdims=True) * over1
    sweep(beside(key_part(0, over0, delta0), key_part(1, over1, delta1)), (none, none))
    give_halves(0)

    empty = jnp.zeros((HD, ROWS), jnp.float32)
    dqt = sweep(beside(query_part(0), query_part(1)), (empty, empty))
    for b in range(2):
        dqs[4 * b : 4 * b + 4] = (dqt[b] * FACTOR).T.astype(jnp.bfloat16).reshape(4, SLICE * GROUP, HD)
    mine_k = give_homes(0)
    dq_copies = []
    for dz in Z_ORDER:
        to = (z + dz) % HEADS
        dq_copies.append(launch(remote(dqs.at[to], dq_in.at[z], dq_send.at[dz], dq_recv.at[dz], head=to)))
    dq_in[z] = dqs[z]
    v_copies = to_tokens(1, mine_v)
    settle()
    k_copies = to_tokens(0, mine_k)

    picks = one_hot(regroup)
    for copy in dq_copies:
        copy.wait_recv()
    for o in range(4):
        moved = dq_in[:, o * 32 : (o + 1) * 32, :].reshape(256, HD)
        gq_ref[o * 256 : (o + 1) * 256, :] = exact_dot(picks, moved)
    picks = one_hot(kv_tokens_first)
    for copy in v_copies:
        copy.wait_recv()
    gv_ref[...] = exact_dot(picks, home_in[1].reshape(256, HD))
    for copy in k_copies:
        copy.wait_recv()
    gk_ref[...] = exact_dot(picks, home_in[0].reshape(256, HD))
    settle()


def store_kernel(gq, gk, gv, gq_out, gk_out, gv_out, sem):
    copies = [
        pltpu.make_async_copy(src, dst, sem.at[i])
        for i, (src, dst) in enumerate(((gq, gq_out), (gk, gk_out), (gv, gv_out)))
    ]
    for copy in copies:
        copy.start()
    for copy in copies:
        copy.wait()


def whole():
    return pl.BlockSpec(memory_space=pltpu.VMEM)


def anywhere():
    return pl.BlockSpec(memory_space=pl.ANY)


def shape(*dims):
    return jax.ShapeDtypeStruct(dims, jnp.bfloat16)


def buffer(*dims, dtype=jnp.bfloat16):
    return pltpu.VMEM(dims, dtype)


def sems(*dims):
    return pltpu.SemaphoreType.DMA(dims)


def local(queries, keys, values, grad_out, ancestry):
    rows = SLICE * GROUP
    results = (shape(SLICE * 32, HD), shape(SLICE * HEADS, HD), shape(SLICE * HEADS, HD))
    grads = pl.pallas_call(
        kernel,
        out_shape=tuple(pltpu.VMEM(r.shape, r.dtype) for r in results),
        in_specs=[anywhere()] * 5,
        out_specs=(whole(),) * 3,
        scratch_shapes=[
            pltpu.SMEM((DEPTH, 2 * NT), jnp.int32),
            buffer(SLICE * 32, HD), buffer(SLICE * HEADS, HD), buffer(SLICE * HEADS, HD), buffer(SLICE * 32, HD),
            sems(5),
            buffer(HEADS, SLICE, HD), buffer(HEADS, SLICE, HD), buffer(HEADS, rows, HD), buffer(HEADS, rows, HD),
            buffer(HEADS, rows, HD), buffer(HEADS, rows, HD), buffer(POOL, BLK, HD), buffer(POOL, BLK, HD),
            pltpu.SMEM((2, SLOTS), jnp.int32), pltpu.SMEM((2, POOL), jnp.int32),
            buffer(KEYS, ROWS, dtype=jnp.float32), buffer(KEYS, ROWS, dtype=jnp.float32),
            buffer(KEYS, ROWS, dtype=jnp.float32), buffer(KEYS, ROWS, dtype=jnp.float32),
            buffer(KEYS, ROWS), buffer(KEYS, ROWS),
            buffer(2, SLOTS + 1, BLK, HD, dtype=jnp.float32),
            buffer(NX * NY, BLK, HD), buffer(NX * NY, BLK, HD),
            buffer(2, NX, NY, BLK, HD), buffer(2, NX, NY, BLK, HD), buffer(2, NX, NY, BLK, HD),
            buffer(2, HEADS, SLICE, HD), buffer(2, HEADS, SLICE, HD), buffer(HEADS, rows, HD), buffer(HEADS, rows, HD),
            sems(4, 8), sems(4, 8), sems(2, 4, 4), sems(2, 4, 4), sems(2, 4, 4), sems(2, 4, 4),
            sems(2, 4, 4), sems(2, 4, 4), sems(2, 4, 4), sems(2, 4, 4), sems(2, 8), sems(2, 8), sems(8), sems(8),
        ],
        compiler_params=pltpu.CompilerParams(collective_id=0, has_side_effects=True, vmem_limit_bytes=VMEM_LIMIT),
        name="backward",
    )(
        ancestry.T,
        queries.reshape(SLICE * 32, HD),
        keys.reshape(SLICE * HEADS, HD),
        values.reshape(SLICE * HEADS, HD),
        grad_out.reshape(SLICE * 32, HD),
    )
    gq, gk, gv = pl.pallas_call(
        store_kernel,
        out_shape=results,
        in_specs=[whole()] * 3,
        out_specs=(anywhere(),) * 3,
        scratch_shapes=[sems(3)],
        name="store",
    )(*(pltpu.with_memory_space_constraint(r, pltpu.VMEM) for r in grads))
    return (
        gq.reshape(SLICE, 32, HD),
        gk.reshape(SLICE, HEADS, HD),
        gv.reshape(SLICE, HEADS, HD),
    )


def solution(mesh):
    placed = P(("tok", "head"), None, None)
    return jax.shard_map(
        local,
        mesh=mesh,
        in_specs=(placed, placed, placed, placed, P()),
        out_specs=(placed, placed, placed),
        check_vma=False,
    )
```
